128 devices in a mesh: wide: 32 (over y, z, core), node: 4 (over x).
Axes of the slice: x: 4, y: 4, z: 4, core: 2. Of those that a mesh axis runs over, the one named last changes fastest.
Arguments:
- item_factors: float32 [262144, 256], P('wide', 'node')
- need_owner: int32 [1024, 1], P('wide'), may hold values from 0 to 31; in each aligned block of 32 rows (0 to 31, 32 to 63, ...) at most 2 rows name the same one
- need_slot: int32 [1024], P('wide'), may hold values from 0 to 63
- block_index: int32 [8192], P(('wide', 'node')), may hold values from 0 to 63, as said below
- block_count: int32 [128], P(('wide', 'node')), may hold values from 16 to 64
- weights: float32 [8192, 128, 128], P(('wide', 'node')), may hold values from 1 to 40
- user_old: float32 [32768, 256], P(('wide', 'node')), may hold values from -2 to 2
Outputs:
- users_new: float32 [32768, 256], P(('wide', 'node'))
- user_gram: float32 [256, 256], replicated
- at_owners: float32 [32, 32, 1024, 256], P('wide', None, 'node')
The draws below stay inside these ranges and needn't reach their ends.
Inputs may be any that keep to these rules, and one draw needn't show every extreme that they name: `need_owner`: within the 32 entries of one group, no item group is named by more than 2 entries. `block_index`: the 64 entries of one device are all different.
All inputs are finite; a program needn't handle non-finite values.
Results may differ from the reference program's by a relative error of at most 0.0003.
Values sent between devices are 32-bit elements; how exact they have to be, the bound alone decides.
A program may use at most 128 MiB of HBM per device.

```python
import math
import jax
import jax.numpy as jnp
import numpy as np
from jax import lax

K = 256
TILE = 128
ITERS = 2
U_DEV = 256
NEED = 32
NB = 64
TILES_W = 64
MOST = 2
USERS = 32768
LISTS = 1024
BLOCKS = 8192
N_WIDE = 32
N_NODE = 4


def draw_item_factors(key, part):
    key = jax.random.fold_in(key, 11)
    scale_key, value_key = jax.random.split(key, 2)
    column_scale = 0.003 * 10.0 ** jax.random.uniform(scale_key, (K,), jnp.float32)
    values = jax.random.normal(value_key, (N_WIDE * TILES_W * TILE, K), jnp.float32)
    return values * column_scale[None, :]


def draw_block_index(key, part):
    key = jax.random.fold_in(key, 12)
    device_keys = jax.random.split(key, N_WIDE * N_NODE)
    chosen_blocks = jax.vmap(lambda single: jax.random.permutation(single, U_DEV // TILE * NEED)[:NB])(device_keys)
    return chosen_blocks.reshape(-1).astype(jnp.int32)


def draw_block_count(key, part):
    key = jax.random.fold_in(key, 13)
    first_key, second_key = jax.random.split(key)
    devices = N_WIDE * N_NODE
    counts = jax.random.randint(first_key, (devices,), NB // 4, NB + 1)
    fullest = jax.random.randint(second_key, (), 0, devices)
    return jnp.where(jnp.arange(devices) == fullest, NB, counts).astype(jnp.int32)


def touch_ends(values, stream_key, low, largest):
    extent = values.shape
    place = [jax.random.randint(jax.random.fold_in(stream_key, axis), (), 0, extent[axis]) for axis in range(len(extent))]
    values = values.at[tuple(place)].set(low)
    longest = extent.index(max(extent))
    place[longest] = (place[longest] + 1) % extent[longest]
    return values.at[tuple(place)].set(largest)


def steps_of(stream_key, dims, shards, least, top_value):
    def one(axis_at, parts):
        heights = jax.random.uniform(jax.random.fold_in(jax.random.fold_in(stream_key, 6), axis_at), (parts,), jnp.float32, least / len(shards), top_value / len(shards))
        return jnp.repeat(jnp.exp(heights), dims[axis_at] // parts).reshape((-1,) + (1,) * (len(dims) - axis_at - 1))

    gain = one(*shards[0])
    for cut in shards[1:]:
        gain = gain * one(*cut)
    return gain


def deal_out(key, own, number, rows, amount, top, reach, slope):
    sequence = jax.random.permutation(key, amount)
    heavy_load, common = portions_of(amount, rows * top, reach, slope, True), portions_of(amount, rows * top, reach, slope, False)
    places = jnp.arange(amount)

    def named(lengths, turn):
        used = int((lengths > 0).sum())
        fixed = max(1, used // 4)
        moved = fixed + (places - fixed + turn * (used - fixed)) % max(1, amount - fixed)
        return jnp.zeros((amount,), jnp.int32).at[sequence[jnp.where(places < fixed, places, moved)]].set(jnp.asarray(lengths, jnp.int32))

    lengths = jnp.where(number % 4 == 0, named(heavy_load, number // 4), named(common, number - number // 4 - 1))
    mixed = jax.random.permutation(jax.random.fold_in(own, 3), amount)
    giver, receiver = mixed[0:amount // 2 * 2:2], mixed[1:amount // 2 * 2:2]
    margin = jnp.minimum(lengths[giver] - 1, reach - lengths[receiver]) // 2
    margin = jnp.where((giver == sequence[0]) | (receiver == sequence[0]) | (lengths[receiver] == 0), 0, jnp.maximum(margin, 0))
    moved = jax.random.randint(jax.random.fold_in(own, 4), (amount // 2,), 0, 1 << 20) % (margin + 1)
    lengths = lengths.at[giver].add(-moved).at[receiver].add(moved)
    items = jnp.searchsorted(jnp.cumsum(lengths), jnp.arange(rows * top), side="right").astype(jnp.int32)
    table = items.reshape(top, rows).T
    table = table[jax.random.permutation(jax.random.fold_in(own, 1), rows)]
    turn = jax.random.randint(jax.random.fold_in(own, 2), (rows, 1), 0, top)
    return jnp.take_along_axis(table, (jnp.arange(top)[None, :] + turn) % top, axis=1)


def portions_of(number_of, total, most, lean, full):
    portions = [(1 << 20) // math.isqrt(rank ** lean) + 1 for rank in range(1, number_of + 1)]
    largest = most if full else min(most, max(-(-total // number_of), total * portions[0] // sum(portions)))
    least = 1 if total - largest >= number_of - 1 else 0
    holding, spare = [largest] + [least] * (number_of - 1), total - largest - least * (number_of - 1)
    while spare > 0:
        free = [i for i in range(1, number_of) if holding[i] < largest] or [i for i in range(1, number_of) if holding[i] < most]
        whole, left = sum([portions[i] for i in free]), spare
        for i in free:
            extra = min(most - holding[i], max(1, left * portions[i] // whole), spare)
            holding[i] = holding[i] + extra
            spare = spare - extra
    return np.array(holding)


def bell_draw(rng, extent, scale, limit, cuts=(), kind=jnp.bfloat16):
    loudness = steps_of(rng, extent, cuts, -0.22, 0.18) if cuts else 1.0
    drawn = jax.random.normal(rng, extent, jnp.float32) * scale * loudness
    return jnp.minimum(jnp.maximum(drawn, -limit), limit).astype(kind)


def setup_inputs(seed: int = 0) -> dict:
    key_of = jax.random.split(jax.random.key(seed), 8)
    item_factors = draw_item_factors(jax.random.fold_in(key_of[7], 71), 0)
    need_owner_keys = jax.random.split(jax.random.fold_in(key_of[1], 1), LISTS // NEED)
    need_owner_turns = jax.random.permutation(jax.random.fold_in(key_of[1], 3), LISTS // NEED)
    need_owner = jax.vmap(lambda own, number: deal_out(jax.random.fold_in(key_of[1], 2), own, number, NEED, N_WIDE, 1, MOST, 2))(need_owner_keys, need_owner_turns).reshape((LISTS, 1))
    need_slot = touch_ends(jax.random.randint(key_of[2], (LISTS,), 0, TILES_W), jax.random.fold_in(key_of[2], 1), 0, TILES_W - 1).astype(jnp.int32)
    block_index = draw_block_index(jax.random.fold_in(key_of[7], 71), 0)
    block_count = draw_block_count(jax.random.fold_in(key_of[7], 71), 0)
    weights = jnp.clip(jnp.exp(math.log(40.0) - 3.6888795 * jax.random.uniform(key_of[5], (BLOCKS, TILE, TILE), jnp.float32) ** steps_of(key_of[5], (BLOCKS, TILE, TILE), ((0, 128),), -0.2, 0.2)), 1.0, 40.0)
    user_old = bell_draw(key_of[6], (USERS, K), 0.3, 2.0, ((0, 128),), jnp.float32)
    return {"item_factors": item_factors, "need_owner": need_owner, "need_slot": need_slot, "block_index": block_index, "block_count": block_count, "weights": weights, "user_old": user_old}


highest = lax.Precision.HIGHEST
ridge = 1.0
tiny_eps = 1e-6


def operate(direction, item_gram, picked_tiles, live_weights, tile_of_block, block_hot):
    picked = direction[tile_of_block]
    scores = jnp.einsum("btk,bik->bti", picked, picked_tiles, precision=highest)
    spread = jnp.einsum("bti,bik->btk", scores * live_weights, picked_tiles, precision=highest)
    local_term = jnp.einsum("bu,btk->utk", block_hot, spread, precision=highest)
    flat_rows = direction.reshape(-1, direction.shape[2])
    global_part = jnp.dot(flat_rows, item_gram, precision=highest) + ridge * flat_rows
    return global_part.reshape(direction.shape) + local_term


def solve_users(user_block, list_tiles, block_weights, index_list, count, item_gram):
    tiles_per_user = user_block.shape[0] // TILE
    rank_width = user_block.shape[1]
    tile_of_block = index_list // NEED
    list_position = index_list % NEED
    picked_tiles = list_tiles[list_position]
    live_mask = (jnp.arange(index_list.shape[0], dtype=jnp.int32) < count).astype(jnp.float32)
    live_weights = block_weights * live_mask[:, None, None]
    block_hot = (tile_of_block[:, None] == jnp.arange(tiles_per_user, dtype=jnp.int32)[None, :]).astype(jnp.float32)
    pulled = jnp.einsum("bti,bik->btk", live_weights + live_mask[:, None, None], picked_tiles, precision=highest)
    target = jnp.einsum("bu,btk->utk", block_hot, pulled, precision=highest)
    current = user_block.reshape(tiles_per_user, TILE, rank_width)
    residual = target - operate(current, item_gram, picked_tiles, live_weights, tile_of_block, block_hot)
    direction = residual
    norm_sq = jnp.sum(residual * residual, axis=2, keepdims=True)
    for iteration in range(ITERS):
        applied = operate(direction, item_gram, picked_tiles, live_weights, tile_of_block, block_hot)
        curvature = jnp.sum(direction * applied, axis=2, keepdims=True)
        step_size = norm_sq / (curvature + tiny_eps)
        current = current + step_size * direction
        residual = residual - step_size * applied
        norm_next = jnp.sum(residual * residual, axis=2, keepdims=True)
        direction = residual + (norm_next / (norm_sq + tiny_eps)) * direction
        norm_sq = norm_next
    return current.reshape(-1, rank_width)


def reference(item_factors, need_owner, need_slot, block_index, block_count, weights, user_old):
    rank_width = item_factors.shape[1]
    item_gram = jnp.dot(item_factors.T, item_factors, precision=highest)
    item_tiles = item_factors.reshape(N_WIDE * TILES_W, TILE, rank_width)
    owners = need_owner.reshape(N_WIDE, NEED)
    slots = need_slot.reshape(N_WIDE, NEED)
    devices = N_WIDE * N_NODE
    index_all = block_index.reshape(devices, NB)
    weight_all = weights.reshape(devices, NB, TILE, TILE)
    users_all = user_old.reshape(devices, U_DEV, rank_width)

    def per_device(device):
        group_index = device // N_NODE
        tile_ids = owners[group_index] * TILES_W + slots[group_index]
        list_tiles = item_tiles[tile_ids]
        return solve_users(users_all[device], list_tiles, weight_all[device], index_all[device], block_count[device], item_gram)

    solved = lax.map(per_device, jnp.arange(devices, dtype=jnp.int32))
    users_new = solved.reshape(-1, rank_width)
    user_gram = jnp.dot(users_new.T, users_new, precision=highest)
    named_owner = jnp.any(owners[:, :, None] == jnp.arange(N_WIDE, dtype=jnp.int32)[None, None, :], axis=1).astype(jnp.float32)
    grouped = solved.reshape(N_WIDE, N_NODE * U_DEV, rank_width)
    at_owners = named_owner.T[:, :, None, None] * grouped[None]
    return users_new, user_gram, at_owners
```

```python
import functools

import jax
import jax.numpy as jnp
from jax import lax
from jax.experimental import pallas as pl
from jax.experimental.pallas import tpu as pltpu
from jax.sharding import PartitionSpec as P

TILE = 128
ITERS = 2
NEED = 32
K = 256
QUARTER = 64
NB = 64
WIDE = 32
NODE = 4
CORES = 2
PLANE = 16
SIDE = 4
TILES = 64
SHARE = 16
PAIRS = NEED // 2
PART = K // PLANE
RIDGE = 1.0
EPS = 1e-06

MESH = pl.DeviceIdType.MESH
F32 = jnp.float32
BF16 = jnp.bfloat16


def split(x):
    high = x.astype(BF16)
    return high, (x - high.astype(F32)).astype(BF16)


def dot3(a, b, contract):
    dims = ((contract[:1], contract[1:]), ((), ()))
    dot = lambda p, q: lax.dot_general(p, q, dims, preferred_element_type=F32)
    return dot(a[0], b[0]) + (dot(a[0], b[1]) + dot(a[1], b[0]))


def place_at():
    wide, node = lax.axis_index("wide"), lax.axis_index("node")
    return wide, node, wide // CORES, lax.rem(wide, CORES)


def remote(src, dst, send, recv, wide, node):
    return pltpu.make_async_remote_copy(
        src_ref=src, dst_ref=dst, send_sem=send, recv_sem=recv, device_id=(wide, node), device_id_type=MESH
    )


def each(low, high, step):
    lax.fori_loop(low, high, lambda i, c: (step(i), c)[1], 0)


def greet():
    wide, node, spot, core = place_at()
    barrier = pltpu.get_barrier_semaphore()

    def to_wide(k):
        pl.semaphore_signal(barrier, inc=1, device_id=(lax.rem(wide + k, WIDE), node), device_id_type=MESH)

    each(1, WIDE, to_wide)
    for dx in range(1, NODE):
        for dc in range(CORES):
            pl.semaphore_signal(
                barrier,
                inc=1,
                device_id=(spot * CORES + lax.rem(core + dc, CORES), lax.rem(node + dx, NODE)),
                device_id_type=MESH,
            )
    pl.semaphore_wait(barrier, WIDE - 1 + (NODE - 1) * CORES)


class Summer:
    def __init__(self, part, total, red, mid, sems):
        self.part, self.total, self.red, self.mid, self.sems = part, total, red, mid, sems
        self.wide, self.node, self.spot, self.core = place_at()
        self.eighth = self.node * CORES + self.core
        self.rows = pl.ds(pl.multiple_of(self.spot * PART, PART), PART)

    def over_plane(self, k, stage):
        spot = lax.rem(self.spot + k, PLANE)
        send, recv = self.sems.at[stage, 0, k], self.sems.at[stage, 1, k]
        if stage == 0:
            src = self.part.at[pl.ds(pl.multiple_of(spot * PART, PART), PART)]
            dst = self.red.at[self.spot]
        else:
            src = dst = self.total.at[self.rows]
        return remote(src, dst, send, recv, spot * CORES + self.core, self.node)

    def over_eight(self, k):
        other = lax.rem(self.eighth + k, NODE * CORES)
        slot = self.mid.at[self.eighth]
        wide = self.spot * CORES + lax.rem(other, CORES)
        return remote(slot, slot, self.sems.at[1, 0, k], self.sems.at[1, 1, k], wide, other // CORES)

    def first(self):
        each(1, PLANE, lambda k: self.over_plane(k, 0).start())
        self.red[self.spot] = self.part[self.rows, :]

    def second(self):
        each(1, PLANE, lambda k: self.over_plane(k, 0).wait_recv())
        total = self.red[0]
        for i in range(1, PLANE):
            total = total + self.red[i]
        self.mid[self.eighth] = total
        each(1, NODE * CORES, lambda k: self.over_eight(k).start())

    def third(self):
        each(1, NODE * CORES, lambda k: self.over_eight(k).wait_recv())
        total = self.mid[0]
        for i in range(1, NODE * CORES):
            total = total + self.mid[i]
        self.total[self.rows, :] = total
        each(1, PLANE, lambda k: self.over_plane(k, 2).start())

    def last(self):
        each(1, PLANE, lambda k: self.over_plane(k, 2).wait_recv())
        each(1, PLANE, lambda k: self.over_plane(k, 0).wait_send())
        each(1, NODE * CORES, lambda k: self.over_eight(k).wait_send())
        each(1, PLANE, lambda k: self.over_plane(k, 2).wait_send())


SUMMER_SCRATCH = [
    pltpu.VMEM((K, K), F32),
    pltpu.VMEM((PLANE, PART, K), F32),
    pltpu.VMEM((NODE * CORES, PART, K), F32),
    pltpu.SemaphoreType.DMA((3, 2, PLANE)),
]


def plan_kernel(owner, slot, index, count, req, place, where, seen):
    def clear(i):
        req[i] = -1
        where[i] = -1

    def clear_rest(i):
        req[i] = -1

    each(0, NB, clear)
    each(NB, TILE, clear_rest)
    each(0, WIDE, lambda i: seen.__setitem__(i, 0))

    def entry(e):
        o = owner[e]
        at = 2 * o + seen[o]
        seen[o] = seen[o] + 1
        place[e] = at
        req[at] = slot[e]

    each(0, NEED, entry)

    def block(b):
        where[index[b]] = b

    each(0, count[0], block)


def plan(owner, slot, index, count):
    smem = pl.BlockSpec(memory_space=pltpu.SMEM)
    return pl.pallas_call(
        plan_kernel,
        out_shape=[
            jax.ShapeDtypeStruct((TILE,), jnp.int32),
            jax.ShapeDtypeStruct((NEED,), jnp.int32),
            jax.ShapeDtypeStruct((NB,), jnp.int32),
        ],
        in_specs=[smem] * 4,
        out_specs=[smem] * 3,
        scratch_shapes=[pltpu.SMEM((WIDE,), jnp.int32)],
        name="plan",
    )(owner, slot, index, count)


def fetch_kernel(
    item, req, place, lists, gram, table,
    tiles, full, outbox, inbox, asked, part, red, mid, sum_sems, row_sems, ask_sems, tile_sems, ring_sems, load_sems, local_sem,
):
    wide, node, spot, core = place_at()

    def load(t):
        return pltpu.make_async_copy(
            item.at[:, pl.ds(pl.multiple_of(t * TILE, TILE), TILE)], tiles.at[t], load_sems.at[t]
        )

    each(0, TILES, lambda t: load(t).start())
    greet()

    def quarter(x):
        return pl.ds(pl.multiple_of(x * QUARTER, QUARTER), QUARTER)

    def share(x):
        return pl.ds(pl.multiple_of(x * SHARE, SHARE), SHARE)

    def rows_to(dx):
        x = lax.rem(node + dx, NODE)
        return remote(
            tiles.at[share(x)], full.at[:, quarter(node), :], row_sems.at[0, dx], row_sems.at[1, dx], wide, x
        )

    def ask(k):
        return remote(
            req, table.at[wide], ask_sems.at[0, k], ask_sems.at[1, k], lax.rem(wide + k, WIDE), node
        )

    def serve(k):
        other = lax.rem(wide + k, WIDE)
        return remote(
            outbox.at[other], inbox.at[pl.ds(2 * wide, 2)], tile_sems.at[0, k], tile_sems.at[1, k], other, node
        )

    each(1, WIDE, lambda k: ask(k).start())
    each(0, TILES, lambda t: load(t).wait())
    for dx in (1, 3, 2):
        rows_to(dx).start()
    table[wide] = req[...]
    full[:, quarter(node), :] = tiles[share(node)]
    each(1, WIDE, lambda k: ask(k).wait_recv())
    to_scalars = pltpu.make_async_copy(table, asked, local_sem)
    to_scalars.start()
    to_scalars.wait()

    def tile(other, r):
        return tiles[jnp.maximum(asked[other, 0, 2 * wide + r], 0)]

    def fill(k):
        other = lax.rem(wide + k, WIDE)
        for r in range(2):
            outbox[other, r] = tile(other, r)
        serve(k).start()

    each(1, WIDE, fill)
    for r in range(2):
        inbox[2 * wide + r] = tile(wide, r)

    for dx in (1, 3, 2):
        rows_to(dx).wait_recv()
    part[...] = jnp.zeros_like(part)

    def multiply(i):
        pair = split(jnp.concatenate([full[4 * i + j] for j in range(4)], axis=1))
        part[...] += dot3(pair, pair, (1, 1))

    each(0, SHARE // 4, multiply)
    summer = Summer(part, gram, red, mid, sum_sems)
    summer.first()

    each(1, WIDE, lambda k: serve(k).wait_recv())

    right, left = lax.rem(node + 1, NODE), lax.rem(node + NODE - 1, NODE)

    def pass_on(c, x, way):
        own = x is node
        stage = 0 if own else 1
        here = lists.at[pl.ds(2 * c, 2), quarter(x), :]
        return remote(
            here, here, ring_sems.at[stage, 0, way, c], ring_sems.at[stage, 1, way, c], wide, (right, left)[way]
        )

    def pick(c):
        for j in range(2):
            for r in range(2):
                lists[2 * c + j, quarter(node), r * TILE : (r + 1) * TILE] = inbox[place[4 * c + 2 * j + r]]
        pass_on(c, node, 0).start()
        pass_on(c, node, 1).start()

    each(0, 8, pick)
    summer.second()

    def forward(c):
        pass_on(2 * c, node, 0).wait_recv()
        pass_on(2 * c, left, 0).start()
        pass_on(2 * c + 1, node, 1).wait_recv()
        pass_on(2 * c + 1, right, 1).start()

    each(0, 2, forward)
    summer.third()
    each(2, 4, forward)

    def finish(c):
        pass_on(2 * c, node, 1).wait_recv()
        pass_on(2 * c + 1, node, 0).wait_recv()
        pass_on(2 * c, left, 0).wait()
        pass_on(2 * c + 1, right, 1).wait()

    each(0, 4, finish)
    summer.last()

    def drain(c):
        pass_on(c, node, 0).wait_send()
        pass_on(c, node, 1).wait_send()

    each(0, 8, drain)
    for dx in (1, 3, 2):
        rows_to(dx).wait_send()
    each(1, WIDE, lambda k: ask(k).wait_send())
    each(1, WIDE, lambda k: serve(k).wait_send())


def fetch(item, req, place):
    vmem = pl.BlockSpec(memory_space=pltpu.VMEM)
    smem = pl.BlockSpec(memory_space=pltpu.SMEM)
    return pl.pallas_call(
        fetch_kernel,
        out_shape=[
            jax.ShapeDtypeStruct((PAIRS, K, 2 * TILE), F32),
            jax.ShapeDtypeStruct((K, K), F32),
            jax.ShapeDtypeStruct((WIDE, 1, TILE), jnp.int32),
        ],
        in_specs=[pl.BlockSpec(memory_space=pl.ANY), vmem, smem],
        out_specs=[vmem, vmem, vmem],
        scratch_shapes=[
            pltpu.VMEM((TILES, QUARTER, TILE), F32),
            pltpu.VMEM((SHARE, K, TILE), F32),
            pltpu.VMEM((WIDE, 2, QUARTER, TILE), F32),
            pltpu.VMEM((2 * WIDE, QUARTER, TILE), F32),
            pltpu.SMEM((WIDE, 1, TILE), jnp.int32),
            *SUMMER_SCRATCH,
            pltpu.SemaphoreType.DMA((2, NODE)),
            pltpu.SemaphoreType.DMA((2, WIDE)),
            pltpu.SemaphoreType.DMA((2, WIDE)),
            pltpu.SemaphoreType.DMA((2, 2, 2, 8)),
            pltpu.SemaphoreType.DMA((TILES,)),
            pltpu.SemaphoreType.DMA,
        ],
        compiler_params=pltpu.CompilerParams(
            collective_id=0, has_side_effects=True, vmem_limit_bytes=40 * 1024 * 1024
        ),
        name="fetch",
    )(item, req, place)


def solve_kernel(lists, weights, user, gram, where, users_new, partial, high, low, dense, spread):
    x = user[...]
    gram_pair = split(gram[...])

    def globally(d, pair):
        return dot3(pair, gram_pair, (1, 0)) + RIDGE * d

    xs = split(x)
    spread[...] = jnp.zeros_like(spread)

    def start(p):
        v = split(lists[p])
        high[p], low[p] = v
        s = dot3(xs, v, (1, 0))
        rows = []
        for u in range(2):
            cols = []
            for r in range(2):
                at = where[u * NEED + 2 * p + r]
                live = jnp.where(at >= 0, 1.0, 0.0).astype(F32)
                c = weights[jnp.maximum(at, 0)] * live
                dense[p, u * TILE : (u + 1) * TILE, r * TILE : (r + 1) * TILE] = c
                cols.append((c + live) - c * s[u * TILE : (u + 1) * TILE, r * TILE : (r + 1) * TILE])
            rows.append(jnp.concatenate(cols, axis=1))
        t = jnp.concatenate(rows, axis=0)
        spread[...] += dot3(split(t), v, (1, 1))

    each(0, PAIRS, start)
    residual = spread[...] - globally(x, xs)
    direction = residual
    norm = jnp.sum(residual * residual, axis=1, keepdims=True)

    pair = split(direction)
    spread[...] = jnp.zeros_like(spread)

    def apply(p):
        v = (high[p], low[p])
        t = dot3(pair, v, (1, 0)) * dense[p]
        spread[...] += dot3(split(t), v, (1, 1))

    each(0, PAIRS, apply)
    applied = spread[...] + globally(direction, pair)
    step = norm / (jnp.sum(direction * applied, axis=1, keepdims=True) + EPS)
    x = x + step * direction
    residual = residual - step * applied
    following = jnp.sum(residual * residual, axis=1, keepdims=True)
    direction = residual + following / (norm + EPS) * direction
    norm = following

    pair = split(direction)
    spread[...] = jnp.zeros_like(spread)

    def curve(p):
        s = dot3(pair, (high[p], low[p]), (1, 0))
        spread[...] += s * s * dense[p]

    each(0, PAIRS, curve)
    bend = spread[...] + direction * globally(direction, pair)
    step = norm / (jnp.sum(bend, axis=1, keepdims=True) + EPS)
    x = x + step * direction
    users_new[...] = x
    pair = split(x)
    partial[...] = dot3(pair, pair, (0, 0))


def solve(lists, weights, user, gram, where):
    vmem = pl.BlockSpec(memory_space=pltpu.VMEM)
    smem = pl.BlockSpec(memory_space=pltpu.SMEM)
    return pl.pallas_call(
        solve_kernel,
        out_shape=[jax.ShapeDtypeStruct((K, K), F32)] * 2,
        in_specs=[vmem] * 4 + [smem],
        out_specs=[vmem] * 2,
        scratch_shapes=[
            pltpu.VMEM((PAIRS, K, 2 * TILE), BF16),
            pltpu.VMEM((PAIRS, K, 2 * TILE), BF16),
            pltpu.VMEM((PAIRS, K, 2 * TILE), F32),
            pltpu.VMEM((K, K), F32),
        ],
        compiler_params=pltpu.CompilerParams(vmem_limit_bytes=40 * 1024 * 1024),
        name="solve",
    )(lists, weights, user, gram, where)


HALF = 128
BIT = 64


def deliver_kernel(
    users, partial, boxes, user_gram, part, red, mid, sum_sems, line_sems, cross_sems, sib_sems, local_sem
):
    wide, node, spot, core = place_at()
    y, z = spot // SIDE, lax.rem(spot, SIDE)
    greet()
    summer = Summer(partial, user_gram, red, mid, sum_sems)
    summer.first()

    def turn(a, d):
        return lax.rem(a + (d + SIDE), SIDE)

    def block(dy, dz):
        return (turn(y, dy) * SIDE + turn(z, dz)) * CORES + core

    def neighbour(axis, way):
        d = 1 if way == 0 else -1
        return block(d, 0) if axis == 0 else block(0, d)

    def rows(half, bit):
        if bit is None:
            return pl.ds(half * HALF, HALF)
        return pl.ds(half * HALF + bit * BIT, BIT)

    def line(half, way, far):
        axis = half
        d = 0 if not far else (-1 if way == 0 else 1)
        at = block(d, 0) if axis == 0 else block(0, d)
        r = rows(half, way if far else None)
        src = users.at[r] if not far else boxes.at[at, r]
        return remote(
            src, boxes.at[at, r], line_sems.at[0, half, way, far], line_sems.at[1, half, way, far],
            neighbour(axis, way), node,
        )

    def cross(half, along, way, far):
        axis = 1 - half
        d = 0 if not far else (-1 if way == 0 else 1)
        at = block(along, d) if axis == 1 else block(d, along)
        r = rows(half, way if far else None)
        src = users.at[r] if (not far and along == 0) else boxes.at[at, r]
        return remote(
            src, boxes.at[at, r],
            cross_sems.at[0, half, along % SIDE, way, far], cross_sems.at[1, half, along % SIDE, way, far],
            neighbour(axis, way), node,
        )

    def sibling(half, along, over):
        at = block(along, over) if half == 0 else block(over, along)
        r = rows(half, None)
        src = users.at[r] if (along == 0 and over == 0) else boxes.at[at, r]
        i = (along % SIDE) * SIDE + over % SIDE
        return remote(
            src, boxes.at[at, r], sib_sems.at[0, half, i], sib_sems.at[1, half, i],
            spot * CORES + 1 - core, node,
        )

    own = pltpu.make_async_copy(users, boxes.at[wide], local_sem)
    own.start()
    for half in range(2):
        for way in range(2):
            line(half, way, 0).start()
    for half in range(2):
        for way in range(2):
            cross(half, 0, way, 0).start()
    for half in range(2):
        sibling(half, 0, 0).start()

    def come_from(way):
        return -1 if way == 0 else 1

    for way in range(2):
        for half in range(2):
            line(half, way, 0).wait_recv()
            line(half, way, 1).start()
            for w in range(2):
                cross(half, come_from(way), w, 0).start()
            sibling(half, come_from(way), 0).start()
    summer.second()
    for half in range(2):
        for way in range(2):
            line(half, way, 1).wait_recv()
        for w in range(2):
            cross(half, 2, w, 0).start()
        sibling(half, 2, 0).start()
    summer.third()
    for along in (0, -1, 1, 2):
        for half in range(2):
            for way in range(2):
                cross(half, along, way, 0).wait_recv()
                cross(half, along, way, 1).start()
                sibling(half, along, come_from(way)).start()
    summer.last()
    for along in (0, -1, 1, 2):
        for half in range(2):
            for way in range(2):
                cross(half, along, way, 1).wait_recv()
            sibling(half, along, 2).start()
    for along in (0, -1, 1, 2):
        for half in range(2):
            for over in (0, -1, 1, 2):
                sibling(half, along, over).wait()
            for way in range(2):
                for far in range(2):
                    cross(half, along, way, far).wait_send()
    for half in range(2):
        for way in range(2):
            for far in range(2):
                line(half, way, far).wait_send()
    own.wait()


def deliver(users, partial):
    vmem = pl.BlockSpec(memory_space=pltpu.VMEM)
    return pl.pallas_call(
        deliver_kernel,
        out_shape=[
            jax.ShapeDtypeStruct((WIDE, K, K), F32),
            jax.ShapeDtypeStruct((K, K), F32),
        ],
        in_specs=[vmem, vmem],
        out_specs=[pl.BlockSpec(memory_space=pl.ANY), vmem],
        scratch_shapes=[
            *SUMMER_SCRATCH,
            pltpu.SemaphoreType.DMA((2, 2, 2, 2)),
            pltpu.SemaphoreType.DMA((2, 2, SIDE, 2, 2)),
            pltpu.SemaphoreType.DMA((2, 2, PLANE)),
            pltpu.SemaphoreType.DMA,
        ],
        compiler_params=pltpu.CompilerParams(collective_id=1, has_side_effects=True),
        name="deliver",
    )(users, partial)


def mask_kernel(table, boxes, out):
    wide = lax.axis_index("wide")
    for j in range(4):
        named = table[pl.program_id(0) * 4 + j, 0, 2 * wide] >= 0
        out[0, j] = jnp.where(named, boxes[j], 0.0)


def mask(table, boxes):
    return pl.pallas_call(
        mask_kernel,
        grid=(WIDE // 4,),
        out_shape=jax.ShapeDtypeStruct((1, WIDE, K, K), F32),
        in_specs=[pl.BlockSpec(memory_space=pltpu.SMEM), pl.BlockSpec((4, K, K), lambda g: (g, 0, 0))],
        out_specs=pl.BlockSpec((1, 4, K, K), lambda g: (0, g, 0, 0)),
        name="mask",
    )(table, boxes)


def body(item_factors, need_owner, need_slot, block_index, block_count, weights, user_old):
    req, place, where = plan(need_owner[:, 0], need_slot, block_index, block_count)
    lists, gram, table = fetch(item_factors.T, req.reshape(1, TILE), place)
    users_new, partial = solve(lists, weights, user_old, gram, where)
    boxes, user_gram = deliver(users_new, partial)
    return users_new, user_gram, mask(table, boxes)


def solution(mesh):
    placed = (
        P("wide", "node"),
        P("wide", None),
        P("wide"),
        P(("wide", "node")),
        P(("wide", "node")),
        P(("wide", "node"), None, None),
        P(("wide", "node"), None),
    )
    return jax.shard_map(
        body,
        mesh=mesh,
        in_specs=placed,
        out_specs=(P(("wide", "node"), None), P(), P("wide", None, "node", None)),
        check_vma=False,
    )
```

```python
import functools

import jax
import jax.numpy as jnp
from jax import lax
from jax.experimental import pallas as pl
from jax.experimental.pallas import tpu as pltpu
from jax.sharding import PartitionSpec as P

TILE = 128
ITERS = 2
NEED = 32
K = 256
QUARTER = 64
NB = 64
WIDE = 32
NODE = 4
CORES = 2
PLANE = 16
SIDE = 4
TILES = 64
SHARE = 16
PAIRS = NEED // 2
GROUP = 4
STEPS = PAIRS // GROUP
SPAN = GROUP * 2 * TILE
HALF = 128
BIT = 64
PART = K // PLANE
RIDGE = 1.0
EPS = 1e-06

MESH = pl.DeviceIdType.MESH
F32 = jnp.float32
BF16 = jnp.bfloat16


def split(x):
    high = x.astype(BF16)
    return high, (x - high.astype(F32)).astype(BF16)


def dot(a, b, contract):
    return lax.dot_general(a, b, ((contract[:1], contract[1:]), ((), ())), preferred_element_type=F32)


def dot3(a, b, contract):
    left = jnp.concatenate([a[0], a[0], a[1]], axis=contract[0])
    right = jnp.concatenate([b[0], b[1], b[0]], axis=contract[1])
    return dot(left, right, contract)


def place_at():
    wide, node = lax.axis_index("wide"), lax.axis_index("node")
    return wide, node, wide // CORES, lax.rem(wide, CORES)


def remote(src, dst, send, recv, wide, node):
    return pltpu.make_async_remote_copy(
        src_ref=src, dst_ref=dst, send_sem=send, recv_sem=recv, device_id=(wide, node), device_id_type=MESH
    )


def each(low, high, step):
    lax.fori_loop(low, high, lambda i, c: (step(i), c)[1], 0)


def greet():
    wide, node, spot, core = place_at()
    barrier = pltpu.get_barrier_semaphore()

    def to_wide(k):
        pl.semaphore_signal(barrier, inc=1, device_id=(lax.rem(wide + k, WIDE), node), device_id_type=MESH)

    each(1, WIDE, to_wide)
    for dx in range(1, NODE):
        for dc in range(CORES):
            pl.semaphore_signal(
                barrier,
                inc=1,
                device_id=(spot * CORES + lax.rem(core + dc, CORES), lax.rem(node + dx, NODE)),
                device_id_type=MESH,
            )
    pl.semaphore_wait(barrier, WIDE - 1 + (NODE - 1) * CORES)


class Summer:
    def __init__(self, part, total, red, mid, sems):
        self.part, self.total, self.red, self.mid, self.sems = part, total, red, mid, sems
        self.wide, self.node, self.spot, self.core = place_at()
        self.eighth = self.node * CORES + self.core
        self.rows = pl.ds(pl.multiple_of(self.spot * PART, PART), PART)

    def over_plane(self, k, stage):
        spot = lax.rem(self.spot + k, PLANE)
        send, recv = self.sems.at[stage, 0, k], self.sems.at[stage, 1, k]
        if stage == 0:
            src = self.part.at[pl.ds(pl.multiple_of(spot * PART, PART), PART)]
            dst = self.red.at[self.spot]
        else:
            src = dst = self.total.at[self.rows]
        return remote(src, dst, send, recv, spot * CORES + self.core, self.node)

    def over_eight(self, k):
        other = lax.rem(self.eighth + k, NODE * CORES)
        slot = self.mid.at[self.eighth]
        wide = self.spot * CORES + lax.rem(other, CORES)
        return remote(slot, slot, self.sems.at[1, 0, k], self.sems.at[1, 1, k], wide, other // CORES)

    def first(self):
        each(1, PLANE, lambda k: self.over_plane(k, 0).start())
        self.red[self.spot] = self.part[self.rows, :]

    def second(self):
        each(1, PLANE, lambda k: self.over_plane(k, 0).wait_recv())
        total = self.red[0]
        for i in range(1, PLANE):
            total = total + self.red[i]
        self.mid[self.eighth] = total
        each(1, NODE * CORES, lambda k: self.over_eight(k).start())

    def third(self):
        each(1, NODE * CORES, lambda k: self.over_eight(k).wait_recv())
        total = self.mid[0]
        for i in range(1, NODE * CORES):
            total = total + self.mid[i]
        self.total[self.rows, :] = total
        each(1, PLANE, lambda k: self.over_plane(k, 2).start())

    def last(self):
        each(1, PLANE, lambda k: self.over_plane(k, 2).wait_recv())
        each(1, PLANE, lambda k: self.over_plane(k, 0).wait_send())
        each(1, NODE * CORES, lambda k: self.over_eight(k).wait_send())
        each(1, PLANE, lambda k: self.over_plane(k, 2).wait_send())


def plan_kernel(owner, slot, index, count, req, place, where, seen):
    def clear(i):
        req[i] = -1
        where[i] = -1

    def clear_rest(i):
        req[i] = -1

    each(0, NB, clear)
    each(NB, TILE, clear_rest)
    each(0, WIDE, lambda i: seen.__setitem__(i, 0))

    def entry(e):
        o = owner[e]
        at = 2 * o + seen[o]
        seen[o] = seen[o] + 1
        place[e] = at
        req[at] = slot[e]

    each(0, NEED, entry)

    def block(b):
        where[index[b]] = b

    each(0, count[0], block)


def plan(owner, slot, index, count):
    smem = pl.BlockSpec(memory_space=pltpu.SMEM)
    return pl.pallas_call(
        plan_kernel,
        out_shape=[
            jax.ShapeDtypeStruct((TILE,), jnp.int32),
            jax.ShapeDtypeStruct((NEED,), jnp.int32),
            jax.ShapeDtypeStruct((NB,), jnp.int32),
        ],
        in_specs=[smem] * 4,
        out_specs=[smem] * 3,
        scratch_shapes=[pltpu.SMEM((WIDE,), jnp.int32)],
        name="plan",
    )(owner, slot, index, count)


def step_kernel(
    item, req, place, where, weights_in, user_in,
    users_new, user_gram, boxes, table,
    tiles, full, outbox, inbox, asked, lists, weights, user, users, gram, part, red, mid, high, low, dense, spread,
    sum_sems, row_sems, ask_sems, tile_sems, ring_sems, line_sems, cross_sems, sib_sems,
    load_sems, bring_sems, own_sems, local_sem,
):
    wide, node, spot, core = place_at()

    def load(t):
        return pltpu.make_async_copy(
            item.at[:, pl.ds(pl.multiple_of(t * TILE, TILE), TILE)], tiles.at[t], load_sems.at[t]
        )

    each(0, TILES, lambda t: load(t).start())
    bring_weights = pltpu.make_async_copy(weights_in, weights, bring_sems.at[0])
    bring_user = pltpu.make_async_copy(user_in, user, bring_sems.at[1])
    bring_weights.start()
    bring_user.start()
    greet()

    def quarter(x):
        return pl.ds(pl.multiple_of(x * QUARTER, QUARTER), QUARTER)

    def share(x):
        return pl.ds(pl.multiple_of(x * SHARE, SHARE), SHARE)

    def rows_to(dx):
        x = lax.rem(node + dx, NODE)
        return remote(
            tiles.at[share(x)], full.at[:, quarter(node), :], row_sems.at[0, dx], row_sems.at[1, dx], wide, x
        )

    def ask(k):
        return remote(
            req, table.at[wide], ask_sems.at[0, k], ask_sems.at[1, k], lax.rem(wide + k, WIDE), node
        )

    def serve(k):
        other = lax.rem(wide + k, WIDE)
        return remote(
            outbox.at[other], inbox.at[pl.ds(2 * wide, 2)], tile_sems.at[0, k], tile_sems.at[1, k], other, node
        )

    each(1, WIDE, lambda k: ask(k).start())
    each(0, TILES, lambda t: load(t).wait())
    for dx in (1, 3, 2):
        rows_to(dx).start()
    table[wide] = req[...]
    full[:, quarter(node), :] = tiles[share(node)]
    each(1, WIDE, lambda k: ask(k).wait_recv())
    to_scalars = pltpu.make_async_copy(table, asked, local_sem)
    to_scalars.start()
    to_scalars.wait()

    def tile(other, r):
        return tiles[jnp.maximum(asked[other, 0, 2 * wide + r], 0)]

    def fill(k):
        other = lax.rem(wide + k, WIDE)
        for r in range(2):
            outbox[other, r] = tile(other, r)
        serve(k).start()

    each(1, WIDE, fill)
    for r in range(2):
        inbox[2 * wide + r] = tile(wide, r)

    for dx in (1, 3, 2):
        rows_to(dx).wait_recv()
    part[...] = jnp.zeros_like(part)

    def multiply(i):
        pair = split(jnp.concatenate([full[4 * i + j] for j in range(4)], axis=1))
        part[...] += dot3(pair, pair, (1, 1))

    each(0, SHARE // 4, multiply)
    summer = Summer(part, gram, red.at[0], mid.at[0], sum_sems.at[0])
    summer.first()

    each(1, WIDE, lambda k: serve(k).wait_recv())

    right, left = lax.rem(node + 1, NODE), lax.rem(node + NODE - 1, NODE)

    def pass_on(c, x, way):
        own = x is node
        stage = 0 if own else 1
        here = lists.at[pl.ds(2 * c, 2), quarter(x), :]
        return remote(
            here, here, ring_sems.at[stage, 0, way, c], ring_sems.at[stage, 1, way, c], wide, (right, left)[way]
        )

    def pick(c):
        for j in range(2):
            for r in range(2):
                lists[2 * c + j, quarter(node), r * TILE : (r + 1) * TILE] = inbox[place[4 * c + 2 * j + r]]
        pass_on(c, node, 0).start()
        pass_on(c, node, 1).start()

    each(0, 8, pick)
    summer.second()

    def forward(c):
        pass_on(2 * c, node, 0).wait_recv()
        pass_on(2 * c, left, 0).start()
        pass_on(2 * c + 1, node, 1).wait_recv()
        pass_on(2 * c + 1, right, 1).start()

    each(0, 2, forward)
    summer.third()
    each(2, 4, forward)
    bring_weights.wait()
    bring_user.wait()

    x = user[...]
    pair = split(x)
    spread[...] = jnp.zeros_like(spread)

    def arrive(c):
        pass_on(2 * c, node, 1).wait_recv()
        pass_on(2 * c + 1, node, 0).wait_recv()
        pass_on(2 * c, left, 0).wait_recv()
        pass_on(2 * c + 1, right, 1).wait_recv()

    def begin(i):
        arrive(i)
        parts = [split(lists[GROUP * i + j]) for j in range(GROUP)]
        v = tuple(jnp.concatenate([q[k] for q in parts], axis=1) for k in range(2))
        high[i], low[i] = v
        s = dot3(pair, v, (1, 0))
        rows = []
        for u in range(2):
            cols = []
            for r in range(2 * GROUP):
                at = where[u * NEED + 2 * GROUP * i + r]
                live = (jnp.minimum(at, 0) + 1).astype(F32)
                c = weights[jnp.maximum(at, 0)] * live
                here = slice(u * TILE, (u + 1) * TILE), slice(r * TILE, (r + 1) * TILE)
                dense[i, here[0], here[1]] = c
                cols.append((c + live) - c * s[here])
            rows.append(jnp.concatenate(cols, axis=1))
        spread[...] += dot3(split(jnp.concatenate(rows, axis=0)), v, (1, 1))

    each(0, STEPS, begin)
    summer.last()

    gram_pair = split(gram[...])

    def globally(d, pair):
        return dot3(pair, gram_pair, (1, 0)) + RIDGE * d

    residual = spread[...] - globally(x, pair)
    direction = residual
    norm = jnp.sum(residual * residual, axis=1, keepdims=True)

    pair = split(direction)
    spread[...] = jnp.zeros_like(spread)

    def apply(i):
        v = (high[i], low[i])
        t = dot3(pair, v, (1, 0)) * dense[i]
        spread[...] += dot3(split(t), v, (1, 1))

    each(0, STEPS, apply)
    applied = spread[...] + globally(direction, pair)
    step = norm / (jnp.sum(direction * applied, axis=1, keepdims=True) + EPS)
    x = x + step * direction
    residual = residual - step * applied
    following = jnp.sum(residual * residual, axis=1, keepdims=True)
    direction = residual + following / (norm + EPS) * direction
    norm = following

    pair = split(direction)
    spread[...] = direction * globally(direction, pair)

    def curve(i):
        s = dot3(pair, (high[i], low[i]), (1, 0))
        bend = s * s * dense[i]
        total = spread[...]
        for j in range(GROUP):
            total = total + bend[:, j * 2 * TILE : (j + 1) * 2 * TILE]
        spread[...] = total

    each(0, STEPS, curve)
    step = norm / (jnp.sum(spread[...], axis=1, keepdims=True) + EPS)
    x = x + step * direction
    users[...] = x

    y, z = spot // SIDE, lax.rem(spot, SIDE)
    def turn(a, d):
        return lax.rem(a + (d + SIDE), SIDE)

    def block(dy, dz):
        return (turn(y, dy) * SIDE + turn(z, dz)) * CORES + core

    def neighbour(axis, way):
        d = 1 if way == 0 else -1
        return block(d, 0) if axis == 0 else block(0, d)

    def rows(half, bit):
        if bit is None:
            return pl.ds(half * HALF, HALF)
        return pl.ds(half * HALF + bit * BIT, BIT)

    def line(half, way, far):
        axis = half
        d = 0 if not far else (-1 if way == 0 else 1)
        at = block(d, 0) if axis == 0 else block(0, d)
        r = rows(half, way if far else None)
        src = users.at[r] if not far else boxes.at[at, r]
        return remote(
            src, boxes.at[at, r], line_sems.at[0, half, way, far], line_sems.at[1, half, way, far],
            neighbour(axis, way), node,
        )

    def cross(half, along, way, far):
        axis = 1 - half
        d = 0 if not far else (-1 if way == 0 else 1)
        at = block(along, d) if axis == 1 else block(d, along)
        r = rows(half, way if far else None)
        src = users.at[r] if (not far and along == 0) else boxes.at[at, r]
        return remote(
            src, boxes.at[at, r],
            cross_sems.at[0, half, along % SIDE, way, far], cross_sems.at[1, half, along % SIDE, way, far],
            neighbour(axis, way), node,
        )

    def sibling(half, along, over):
        at = block(along, over) if half == 0 else block(over, along)
        r = rows(half, None)
        src = users.at[r] if (along == 0 and over == 0) else boxes.at[at, r]
        i = (along % SIDE) * SIDE + over % SIDE
        return remote(
            src, boxes.at[at, r], sib_sems.at[0, half, i], sib_sems.at[1, half, i],
            spot * CORES + 1 - core, node,
        )

    own = pltpu.make_async_copy(users, boxes.at[wide], own_sems.at[0])
    own.start()
    give = pltpu.make_async_copy(users, users_new, own_sems.at[1])
    give.start()
    for half in range(2):
        for way in range(2):
            line(half, way, 0).start()
    for half in range(2):
        for way in range(2):
            cross(half, 0, way, 0).start()
    for half in range(2):
        sibling(half, 0, 0).start()

    pair = split(x)
    part[...] = dot3(pair, pair, (0, 0))
    summer = Summer(part, user_gram, red.at[1], mid.at[1], sum_sems.at[1])
    summer.first()

    def come_from(way):
        return -1 if way == 0 else 1

    for way in range(2):
        for half in range(2):
            line(half, way, 0).wait_recv()
            line(half, way, 1).start()
            for w in range(2):
                cross(half, come_from(way), w, 0).start()
            sibling(half, come_from(way), 0).start()
    summer.second()
    for half in range(2):
        for way in range(2):
            line(half, way, 1).wait_recv()
        for w in range(2):
            cross(half, 2, w, 0).start()
        sibling(half, 2, 0).start()
    summer.third()
    for along in (0, -1, 1, 2):
        for half in range(2):
            for way in range(2):
                cross(half, along, way, 0).wait_recv()
                cross(half, along, way, 1).start()
                sibling(half, along, come_from(way)).start()
    summer.last()
    for along in (0, -1, 1, 2):
        for half in range(2):
            for way in range(2):
                cross(half, along, way, 1).wait_recv()
            sibling(half, along, 2).start()
    for along in (0, -1, 1, 2):
        for half in range(2):
            for over in (0, -1, 1, 2):
                sibling(half, along, over).wait()
            for way in range(2):
                for far in range(2):
                    cross(half, along, way, far).wait_send()
    for half in range(2):
        for way in range(2):
            for far in range(2):
                line(half, way, far).wait_send()
    own.wait()
    give.wait()

    def drain(c):
        pass_on(c, node, 0).wait_send()
        pass_on(c, node, 1).wait_send()

    each(0, 8, drain)

    def drain_far(c):
        pass_on(2 * c, left, 0).wait_send()
        pass_on(2 * c + 1, right, 1).wait_send()

    each(0, 4, drain_far)
    for dx in (1, 3, 2):
        rows_to(dx).wait_send()
    each(1, WIDE, lambda k: ask(k).wait_send())
    each(1, WIDE, lambda k: serve(k).wait_send())


def step(item, req, place, where, weights, user):
    vmem = pl.BlockSpec(memory_space=pltpu.VMEM)
    smem = pl.BlockSpec(memory_space=pltpu.SMEM)
    hbm = pl.BlockSpec(memory_space=pl.ANY)
    return pl.pallas_call(
        step_kernel,
        out_shape=[
            jax.ShapeDtypeStruct((K, K), F32),
            jax.ShapeDtypeStruct((K, K), F32),
            jax.ShapeDtypeStruct((WIDE, K, K), F32),
            jax.ShapeDtypeStruct((WIDE, 1, TILE), jnp.int32),
        ],
        in_specs=[hbm, vmem, smem, smem, hbm, hbm],
        out_specs=[hbm, vmem, hbm, vmem],
        scratch_shapes=[
            pltpu.VMEM((TILES, QUARTER, TILE), F32),
            pltpu.VMEM((SHARE, K, TILE), F32),
            pltpu.VMEM((WIDE, 2, QUARTER, TILE), F32),
            pltpu.VMEM((2 * WIDE, QUARTER, TILE), F32),
            pltpu.SMEM((WIDE, 1, TILE), jnp.int32),
            pltpu.VMEM((PAIRS, K, 2 * TILE), F32),
            pltpu.VMEM((NB, TILE, TILE), F32),
            pltpu.VMEM((K, K), F32),
            pltpu.VMEM((K, K), F32),
            pltpu.VMEM((K, K), F32),
            pltpu.VMEM((K, K), F32),
            pltpu.VMEM((2, PLANE, PART, K), F32),
            pltpu.VMEM((2, NODE * CORES, PART, K), F32),
            pltpu.VMEM((STEPS, K, SPAN), BF16),
            pltpu.VMEM((STEPS, K, SPAN), BF16),
            pltpu.VMEM((STEPS, K, SPAN), F32),
            pltpu.VMEM((K, K), F32),
            pltpu.SemaphoreType.DMA((2, 3, 2, PLANE)),
            pltpu.SemaphoreType.DMA((2, NODE)),
            pltpu.SemaphoreType.DMA((2, WIDE)),
            pltpu.SemaphoreType.DMA((2, WIDE)),
            pltpu.SemaphoreType.DMA((2, 2, 2, 8)),
            pltpu.SemaphoreType.DMA((2, 2, 2, 2)),
            pltpu.SemaphoreType.DMA((2, 2, SIDE, 2, 2)),
            pltpu.SemaphoreType.DMA((2, 2, PLANE)),
            pltpu.SemaphoreType.DMA((TILES,)),
            pltpu.SemaphoreType.DMA((2,)),
            pltpu.SemaphoreType.DMA((2,)),
            pltpu.SemaphoreType.DMA,
        ],
        compiler_params=pltpu.CompilerParams(
            collective_id=0, has_side_effects=True, vmem_limit_bytes=60 * 1024 * 1024
        ),
        name="step",
    )(item, req, place, where, weights, user)


def mask_kernel(table, boxes, out):
    wide = lax.axis_index("wide")
    for j in range(4):
        named = table[pl.program_id(0) * 4 + j, 0, 2 * wide] >= 0
        out[0, j] = jnp.where(named, boxes[j], 0.0)


def mask(table, boxes):
    return pl.pallas_call(
        mask_kernel,
        grid=(WIDE // 4,),
        out_shape=jax.ShapeDtypeStruct((1, WIDE, K, K), F32),
        in_specs=[pl.BlockSpec(memory_space=pltpu.SMEM), pl.BlockSpec((4, K, K), lambda g: (g, 0, 0))],
        out_specs=pl.BlockSpec((1, 4, K, K), lambda g: (0, g, 0, 0)),
        name="mask",
    )(table, boxes)


def body(item_factors, need_owner, need_slot, block_index, block_count, weights, user_old):
    req, place, where = plan(need_owner[:, 0], need_slot, block_index, block_count)
    users_new, user_gram, boxes, table = step(
        item_factors.T, req.reshape(1, TILE), place, where, weights, user_old
    )
    return users_new, user_gram, mask(table, boxes)


def solution(mesh):
    placed = (
        P("wide", "node"),
        P("wide", None),
        P("wide"),
        P(("wide", "node")),
        P(("wide", "node")),
        P(("wide", "node"), None, None),
        P(("wide", "node"), None),
    )
    return jax.shard_map(
        body,
        mesh=mesh,
        in_specs=placed,
        out_specs=(P(("wide", "node"), None), P(), P("wide", None, "node", None)),
        check_vma=False,
    )
```

```python
import functools

import jax
import jax.numpy as jnp
from jax import lax
from jax.experimental import pallas as pl
from jax.experimental.pallas import tpu as pltpu
from jax.sharding import PartitionSpec as P

TILE = 128
ITERS = 2
NEED = 32
K = 256
QUARTER = 64
RANKS = QUARTER // 2
NB = 64
WIDE = 32
NODE = 4
CORES = 2
PLANE = 16
SIDE = 4
TILES = 64
SHARE = 16
PAIRS = NEED // 2
GROUP = 4
STEPS = PAIRS // GROUP
SPAN = GROUP * 2 * TILE
HALF = 128
BIT = 64
PART = K // PLANE
RIDGE = 1.0
EPS = 1e-06

MESH = pl.DeviceIdType.MESH
F32 = jnp.float32
BF16 = jnp.bfloat16


def split(x):
    high = x.astype(BF16)
    return high, (x - high.astype(F32)).astype(BF16)


def dot(a, b, contract):
    return lax.dot_general(a, b, ((contract[:1], contract[1:]), ((), ())), preferred_element_type=F32)


def dot3(a, b, contract):
    left = jnp.concatenate([a[0], a[0], a[1]], axis=contract[0])
    right = jnp.concatenate([b[0], b[1], b[0]], axis=contract[1])
    return dot(left, right, contract)


def place_at():
    wide, node = lax.axis_index("wide"), lax.axis_index("node")
    return wide, node, wide // CORES, lax.rem(wide, CORES)


def remote(src, dst, send, recv, wide, node):
    return pltpu.make_async_remote_copy(
        src_ref=src, dst_ref=dst, send_sem=send, recv_sem=recv, device_id=(wide, node), device_id_type=MESH
    )


def each(low, high, step):
    lax.fori_loop(low, high, lambda i, c: (step(i), c)[1], 0)


def greet():
    wide, node, spot, core = place_at()
    barrier = pltpu.get_barrier_semaphore()

    def to_wide(k):
        pl.semaphore_signal(barrier, inc=1, device_id=(lax.rem(wide + k, WIDE), node), device_id_type=MESH)

    each(1, WIDE, to_wide)
    for dx in range(1, NODE):
        for dc in range(CORES):
            pl.semaphore_signal(
                barrier,
                inc=1,
                device_id=(spot * CORES + lax.rem(core + dc, CORES), lax.rem(node + dx, NODE)),
                device_id_type=MESH,
            )
    pl.semaphore_wait(barrier, WIDE - 1 + (NODE - 1) * CORES)


class Summer:
    def __init__(self, part, total, red, mid, sems):
        self.part, self.total, self.red, self.mid, self.sems = part, total, red, mid, sems
        self.wide, self.node, self.spot, self.core = place_at()
        self.eighth = self.node * CORES + self.core
        self.rows = pl.ds(pl.multiple_of(self.spot * PART, PART), PART)

    def over_plane(self, k, stage):
        spot = lax.rem(self.spot + k, PLANE)
        send, recv = self.sems.at[stage, 0, k], self.sems.at[stage, 1, k]
        if stage == 0:
            src = self.part.at[pl.ds(pl.multiple_of(spot * PART, PART), PART)]
            dst = self.red.at[self.spot]
        else:
            src = dst = self.total.at[self.rows]
        return remote(src, dst, send, recv, spot * CORES + self.core, self.node)

    def over_eight(self, k):
        other = lax.rem(self.eighth + k, NODE * CORES)
        slot = self.mid.at[self.eighth]
        wide = self.spot * CORES + lax.rem(other, CORES)
        return remote(slot, slot, self.sems.at[1, 0, k], self.sems.at[1, 1, k], wide, other // CORES)

    def first(self):
        each(1, PLANE, lambda k: self.over_plane(k, 0).start())
        self.red[self.spot] = self.part[self.rows, :]

    def second(self):
        each(1, PLANE, lambda k: self.over_plane(k, 0).wait_recv())
        total = self.red[0]
        for i in range(1, PLANE):
            total = total + self.red[i]
        self.mid[self.eighth] = total
        each(1, NODE * CORES, lambda k: self.over_eight(k).start())

    def third(self):
        each(1, NODE * CORES, lambda k: self.over_eight(k).wait_recv())
        total = self.mid[0]
        for i in range(1, NODE * CORES):
            total = total + self.mid[i]
        self.total[self.rows, :] = total
        each(1, PLANE, lambda k: self.over_plane(k, 2).start())

    def last(self):
        each(1, PLANE, lambda k: self.over_plane(k, 2).wait_recv())
        each(1, PLANE, lambda k: self.over_plane(k, 0).wait_send())
        each(1, NODE * CORES, lambda k: self.over_eight(k).wait_send())
        each(1, PLANE, lambda k: self.over_plane(k, 2).wait_send())


def plan_kernel(owner, slot, index, count, req, place, where, seen):
    def clear(i):
        req[i] = -1
        where[i] = -1

    def clear_rest(i):
        req[i] = -1

    each(0, NB, clear)
    each(NB, TILE, clear_rest)
    each(0, WIDE, lambda i: seen.__setitem__(i, 0))

    def entry(e):
        o = owner[e]
        at = 2 * o + seen[o]
        seen[o] = seen[o] + 1
        place[e] = at
        req[at] = slot[e]

    each(0, NEED, entry)

    def block(b):
        where[index[b]] = b

    each(0, count[0], block)


def plan(owner, slot, index, count):
    smem = pl.BlockSpec(memory_space=pltpu.SMEM)
    return pl.pallas_call(
        plan_kernel,
        out_shape=[
            jax.ShapeDtypeStruct((TILE,), jnp.int32),
            jax.ShapeDtypeStruct((NEED,), jnp.int32),
            jax.ShapeDtypeStruct((NB,), jnp.int32),
        ],
        in_specs=[smem] * 4,
        out_specs=[smem] * 3,
        scratch_shapes=[pltpu.SMEM((WIDE,), jnp.int32)],
        name="plan",
    )(owner, slot, index, count)


def step_kernel(
    item, req, place, where, weights_in, user_in,
    users_new, user_gram, boxes, table,
    tiles, full, relay, outbox, inbox_low, inbox_high, asked, lists, weights, user, users, gram, part, red, mid, high, low, dense, spread,
    sum_sems, row_sems, ask_sems, tile_sems, ring_sems, line_sems, cross_sems, sib_sems,
    load_sems, bring_sems, own_sems, local_sem,
):
    wide, node, spot, core = place_at()
    inboxes = inbox_low, inbox_high

    def load(t):
        return pltpu.make_async_copy(
            item.at[:, pl.ds(pl.multiple_of(t * TILE, TILE), TILE)], tiles.at[t], load_sems.at[t]
        )

    each(0, TILES, lambda t: load(t).start())
    bring_weights = pltpu.make_async_copy(weights_in, weights, bring_sems.at[0])
    bring_user = pltpu.make_async_copy(user_in, user, bring_sems.at[1])
    bring_weights.start()
    bring_user.start()
    greet()

    def quarter(x):
        return pl.ds(pl.multiple_of(x * QUARTER, QUARTER), QUARTER)

    def share(x):
        return pl.ds(pl.multiple_of(x * SHARE, SHARE), SHARE)

    right, left = lax.rem(node + 1, NODE), lax.rem(node + NODE - 1, NODE)
    across = lax.rem(node + 2, NODE)

    def part_share(x, way):
        return pl.ds(pl.multiple_of(x * SHARE + way * SHARE // 2, SHARE // 2), SHARE // 2)

    def rows_near(way):
        x = (right, left)[way]
        return remote(
            tiles.at[share(x)], full.at[:, quarter(node), :], row_sems.at[0, 0, way], row_sems.at[1, 0, way], wide, x
        )

    def rows_relay(way):
        return remote(
            tiles.at[part_share(across, way)], relay.at[way],
            row_sems.at[0, 1, way], row_sems.at[1, 1, way], wide, (right, left)[way],
        )

    def rows_far(way):
        return remote(
            relay.at[way], full.at[pl.ds(way * SHARE // 2, SHARE // 2), quarter((left, right)[way]), :],
            row_sems.at[0, 2, way], row_sems.at[1, 2, way], wide, (right, left)[way],
        )

    def ask(k):
        return remote(
            req, table.at[wide], ask_sems.at[0, k], ask_sems.at[1, k], lax.rem(wide + k, WIDE), node
        )

    def serve(k, part):
        other = lax.rem(wide + k, WIDE)
        return remote(
            outbox.at[part, other], inboxes[part].at[pl.ds(2 * wide, 2)],
            tile_sems.at[0, part, k], tile_sems.at[1, part, k], other, node,
        )

    each(1, WIDE, lambda k: ask(k).start())
    each(0, TILES, lambda t: load(t).wait())
    for way in range(2):
        rows_relay(way).start()
    for way in range(2):
        rows_near(way).start()
    table[wide] = req[...]
    full[:, quarter(node), :] = tiles[share(node)]
    each(1, WIDE, lambda k: ask(k).wait_recv())
    to_scalars = pltpu.make_async_copy(table, asked, local_sem)
    to_scalars.start()
    to_scalars.wait()

    def fill(k, part):
        other = lax.rem(wide + k, WIDE)
        for r in range(2):
            at = jnp.maximum(asked[other, 0, 2 * wide + r], 0)
            outbox[part, other, r] = tiles[at, part * RANKS : (part + 1) * RANKS, :]
        serve(k, part).start()

    for part_rank in range(2):
        each(1, WIDE, lambda k, part_rank=part_rank: fill(k, part_rank))
    for r in range(2):
        mine = tiles[jnp.maximum(asked[wide, 0, 2 * wide + r], 0)]
        for half in range(2):
            inboxes[half][2 * wide + r] = mine[half * RANKS : (half + 1) * RANKS]
    for way in range(2):
        rows_relay(way).wait_recv()
        rows_far(way).start()

    def pass_on(c, x, way, half):
        stage = 0 if x is node else 1
        ranks = pl.ds(pl.multiple_of(x * QUARTER + half * RANKS, RANKS), RANKS)
        here = lists.at[pl.ds(GROUP * c, GROUP), ranks, :]
        sems = ring_sems.at[half, stage]
        return remote(here, here, sems.at[0, way, c], sems.at[1, way, c], wide, (right, left)[way])

    def pick(c, half):
        ranks = pl.ds(pl.multiple_of(node * QUARTER + half * RANKS, RANKS), RANKS)
        for j in range(GROUP):
            for r in range(2):
                at = place[2 * GROUP * c + 2 * j + r]
                lists[GROUP * c + j, ranks, r * TILE : (r + 1) * TILE] = inboxes[half][at]
        pass_on(c, node, 0, half).start()
        pass_on(c, node, 1, half).start()

    def forward(c, half):
        pass_on(2 * c, node, 0, half).wait_recv()
        pass_on(2 * c, left, 0, half).start()
        pass_on(2 * c + 1, node, 1, half).wait_recv()
        pass_on(2 * c + 1, right, 1, half).start()

    each(1, WIDE, lambda k: serve(k, 0).wait_recv())
    each(0, STEPS, lambda c: pick(c, 0))
    for way in range(2):
        rows_near(way).wait_recv()
        rows_far(way).wait_recv()
    part[...] = jnp.zeros_like(part)

    def multiply(i):
        pair = split(jnp.concatenate([full[4 * i + j] for j in range(4)], axis=1))
        part[...] += dot3(pair, pair, (1, 1))

    each(0, SHARE // 4, multiply)
    summer = Summer(part, gram, red.at[0], mid.at[0], sum_sems.at[0])
    summer.first()

    each(0, STEPS // 2, lambda c: forward(c, 0))
    each(1, WIDE, lambda k: serve(k, 1).wait_recv())
    each(0, STEPS, lambda c: pick(c, 1))
    summer.second()
    forward(0, 1)
    summer.third()
    forward(1, 1)
    bring_weights.wait()
    bring_user.wait()

    x = user[...]
    pair = split(x)
    spread[...] = jnp.zeros_like(spread)

    def arrive(c, half):
        pass_on(2 * c, node, 1, half).wait_recv()
        pass_on(2 * c + 1, node, 0, half).wait_recv()
        pass_on(2 * c, left, 0, half).wait_recv()
        pass_on(2 * c + 1, right, 1, half).wait_recv()

    each(0, STEPS // 2, lambda c: arrive(c, 0))

    def begin(i):
        parts = [split(lists[GROUP * i + j]) for j in range(GROUP)]
        v = tuple(jnp.concatenate([q[k] for q in parts], axis=1) for k in range(2))
        high[i], low[i] = v
        s = dot3(pair, v, (1, 0))
        rows = []
        for u in range(2):
            cols = []
            for r in range(2 * GROUP):
                at = where[u * NEED + 2 * GROUP * i + r]
                live = (jnp.minimum(at, 0) + 1).astype(F32)
                c = weights[jnp.maximum(at, 0)] * live
                here = slice(u * TILE, (u + 1) * TILE), slice(r * TILE, (r + 1) * TILE)
                dense[i, here[0], here[1]] = c
                cols.append((c + live) - c * s[here])
            rows.append(jnp.concatenate(cols, axis=1))
        spread[...] += dot3(split(jnp.concatenate(rows, axis=0)), v, (1, 1))

    for c in range(STEPS // 2):
        arrive(c, 1)
        each(2 * c, 2 * c + 2, begin)
    summer.last()

    gram_pair = split(gram[...])

    def globally(d, pair):
        return dot3(pair, gram_pair, (1, 0)) + RIDGE * d

    residual = spread[...] - globally(x, pair)
    direction = residual
    norm = jnp.sum(residual * residual, axis=1, keepdims=True)

    pair = split(direction)
    spread[...] = jnp.zeros_like(spread)

    def apply(i):
        v = (high[i], low[i])
        t = dot3(pair, v, (1, 0)) * dense[i]
        spread[...] += dot3(split(t), v, (1, 1))

    each(0, STEPS, apply)
    applied = spread[...] + globally(direction, pair)
    step = norm / (jnp.sum(direction * applied, axis=1, keepdims=True) + EPS)
    x = x + step * direction
    residual = residual - step * applied
    following = jnp.sum(residual * residual, axis=1, keepdims=True)
    direction = residual + following / (norm + EPS) * direction
    norm = following

    pair = split(direction)
    spread[...] = direction * globally(direction, pair)

    def curve(i):
        s = dot3(pair, (high[i], low[i]), (1, 0))
        bend = s * s * dense[i]
        total = spread[...]
        for j in range(GROUP):
            total = total + bend[:, j * 2 * TILE : (j + 1) * 2 * TILE]
        spread[...] = total

    each(0, STEPS, curve)
    step = norm / (jnp.sum(spread[...], axis=1, keepdims=True) + EPS)
    x = x + step * direction
    users[...] = x

    y, z = spot // SIDE, lax.rem(spot, SIDE)
    def turn(a, d):
        return lax.rem(a + (d + SIDE), SIDE)

    def block(dy, dz):
        return (turn(y, dy) * SIDE + turn(z, dz)) * CORES + core

    def neighbour(axis, way):
        d = 1 if way == 0 else -1
        return block(d, 0) if axis == 0 else block(0, d)

    def rows(half, bit):
        if bit is None:
            return pl.ds(half * HALF, HALF)
        return pl.ds(half * HALF + bit * BIT, BIT)

    def line(half, way, far):
        axis = half
        d = 0 if not far else (-1 if way == 0 else 1)
        at = block(d, 0) if axis == 0 else block(0, d)
        r = rows(half, way if far else None)
        src = users.at[r] if not far else boxes.at[at, r]
        return remote(
            src, boxes.at[at, r], line_sems.at[0, half, way, far], line_sems.at[1, half, way, far],
            neighbour(axis, way), node,
        )

    def cross(half, along, way, far):
        axis = 1 - half
        d = 0 if not far else (-1 if way == 0 else 1)
        at = block(along, d) if axis == 1 else block(d, along)
        r = rows(half, way if far else None)
        src = users.at[r] if (not far and along == 0) else boxes.at[at, r]
        return remote(
            src, boxes.at[at, r],
            cross_sems.at[0, half, along % SIDE, way, far], cross_sems.at[1, half, along % SIDE, way, far],
            neighbour(axis, way), node,
        )

    def sibling(half, along, over):
        at = block(along, over) if half == 0 else block(over, along)
        r = rows(half, None)
        src = users.at[r] if (along == 0 and over == 0) else boxes.at[at, r]
        i = (along % SIDE) * SIDE + over % SIDE
        return remote(
            src, boxes.at[at, r], sib_sems.at[0, half, i], sib_sems.at[1, half, i],
            spot * CORES + 1 - core, node,
        )

    own = pltpu.make_async_copy(users, boxes.at[wide], own_sems.at[0])
    own.start()
    give = pltpu.make_async_copy(users, users_new, own_sems.at[1])
    give.start()
    for half in range(2):
        for way in range(2):
            line(half, way, 0).start()
    for half in range(2):
        for way in range(2):
            cross(half, 0, way, 0).start()
    for half in range(2):
        sibling(half, 0, 0).start()

    pair = split(x)
    part[...] = dot3(pair, pair, (0, 0))
    summer = Summer(part, user_gram, red.at[1], mid.at[1], sum_sems.at[1])
    summer.first()

    def come_from(way):
        return -1 if way == 0 else 1

    for way in range(2):
        for half in range(2):
            line(half, way, 0).wait_recv()
            line(half, way, 1).start()
            for w in range(2):
                cross(half, come_from(way), w, 0).start()
            sibling(half, come_from(way), 0).start()
    summer.second()
    for half in range(2):
        for way in range(2):
            line(half, way, 1).wait_recv()
        for w in range(2):
            cross(half, 2, w, 0).start()
        sibling(half, 2, 0).start()
    summer.third()
    for along in (0, -1, 1, 2):
        for half in range(2):
            for way in range(2):
                cross(half, along, way, 0).wait_recv()
                cross(half, along, way, 1).start()
                sibling(half, along, come_from(way)).start()
    summer.last()
    for along in (0, -1, 1, 2):
        for half in range(2):
            for way in range(2):
                cross(half, along, way, 1).wait_recv()
            sibling(half, along, 2).start()
    for along in (0, -1, 1, 2):
        for half in range(2):
            for over in (0, -1, 1, 2):
                sibling(half, along, over).wait()
            for way in range(2):
                for far in range(2):
                    cross(half, along, way, far).wait_send()
    for half in range(2):
        for way in range(2):
            for far in range(2):
                line(half, way, far).wait_send()
    own.wait()
    give.wait()

    for half in range(2):
        for way in range(2):
            each(0, STEPS, lambda c, half=half, way=way: pass_on(c, node, way, half).wait_send())
        for c in range(STEPS // 2):
            pass_on(2 * c, left, 0, half).wait_send()
            pass_on(2 * c + 1, right, 1, half).wait_send()
    for way in range(2):
        rows_relay(way).wait_send()
        rows_near(way).wait_send()
        rows_far(way).wait_send()
    each(1, WIDE, lambda k: ask(k).wait_send())
    for part_rank in range(2):
        each(1, WIDE, lambda k, part_rank=part_rank: serve(k, part_rank).wait_send())


def step(item, req, place, where, weights, user):
    vmem = pl.BlockSpec(memory_space=pltpu.VMEM)
    smem = pl.BlockSpec(memory_space=pltpu.SMEM)
    hbm = pl.BlockSpec(memory_space=pl.ANY)
    return pl.pallas_call(
        step_kernel,
        out_shape=[
            jax.ShapeDtypeStruct((K, K), F32),
            jax.ShapeDtypeStruct((K, K), F32),
            pltpu.VMEM((WIDE, K, K), F32),
            jax.ShapeDtypeStruct((WIDE, 1, TILE), jnp.int32),
        ],
        in_specs=[hbm, vmem, smem, smem, hbm, hbm],
        out_specs=[hbm, vmem, vmem, vmem],
        scratch_shapes=[
            pltpu.VMEM((TILES, QUARTER, TILE), F32),
            pltpu.VMEM((SHARE, K, TILE), F32),
            pltpu.VMEM((2, SHARE // 2, QUARTER, TILE), F32),
            pltpu.VMEM((2, WIDE, 2, RANKS, TILE), F32),
            pltpu.VMEM((2 * WIDE, RANKS, TILE), F32),
            pltpu.VMEM((2 * WIDE, RANKS, TILE), F32),
            pltpu.SMEM((WIDE, 1, TILE), jnp.int32),
            pltpu.VMEM((PAIRS, K, 2 * TILE), F32),
            pltpu.VMEM((NB, TILE, TILE), F32),
            pltpu.VMEM((K, K), F32),
            pltpu.VMEM((K, K), F32),
            pltpu.VMEM((K, K), F32),
            pltpu.VMEM((K, K), F32),
            pltpu.VMEM((2, PLANE, PART, K), F32),
            pltpu.VMEM((2, NODE * CORES, PART, K), F32),
            pltpu.VMEM((STEPS, K, SPAN), BF16),
            pltpu.VMEM((STEPS, K, SPAN), BF16),
            pltpu.VMEM((STEPS, K, SPAN), F32),
            pltpu.VMEM((K, K), F32),
            pltpu.SemaphoreType.DMA((2, 3, 2, PLANE)),
            pltpu.SemaphoreType.DMA((2, 3, 2)),
            pltpu.SemaphoreType.DMA((2, WIDE)),
            pltpu.SemaphoreType.DMA((2, 2, WIDE)),
            pltpu.SemaphoreType.DMA((2, 2, 2, 2, STEPS)),
            pltpu.SemaphoreType.DMA((2, 2, 2, 2)),
            pltpu.SemaphoreType.DMA((2, 2, SIDE, 2, 2)),
            pltpu.SemaphoreType.DMA((2, 2, PLANE)),
            pltpu.SemaphoreType.DMA((TILES,)),
            pltpu.SemaphoreType.DMA((2,)),
            pltpu.SemaphoreType.DMA((2,)),
            pltpu.SemaphoreType.DMA,
        ],
        compiler_params=pltpu.CompilerParams(
            collective_id=0, has_side_effects=True, vmem_limit_bytes=50 * 1024 * 1024
        ),
        name="step",
    )(item, req, place, where, weights, user)


def mask_kernel(table, boxes, out, zeros, sems):
    wide = lax.axis_index("wide")
    zeros[...] = jnp.zeros_like(zeros)

    def begin(g):
        named = table[g, 0, 2 * wide] >= 0

        @pl.when(named)
        def _():
            pltpu.make_async_copy(boxes.at[g], out.at[0, g], sems.at[g]).start()

        @pl.when(jnp.logical_not(named))
        def _():
            pltpu.make_async_copy(zeros, out.at[0, g], sems.at[g]).start()

    each(0, WIDE, begin)
    each(0, WIDE, lambda g: pltpu.make_async_copy(zeros, out.at[0, g], sems.at[g]).wait())


def mask(table, boxes):
    return pl.pallas_call(
        mask_kernel,
        out_shape=jax.ShapeDtypeStruct((1, WIDE, K, K), F32),
        in_specs=[pl.BlockSpec(memory_space=pltpu.SMEM), pl.BlockSpec(memory_space=pltpu.VMEM)],
        out_specs=pl.BlockSpec(memory_space=pl.ANY),
        scratch_shapes=[pltpu.VMEM((K, K), F32), pltpu.SemaphoreType.DMA((WIDE,))],
        compiler_params=pltpu.CompilerParams(vmem_limit_bytes=10 * 1024 * 1024),
        name="mask",
    )(table, boxes)


def body(item_factors, need_owner, need_slot, block_index, block_count, weights, user_old):
    req, place, where = plan(need_owner[:, 0], need_slot, block_index, block_count)
    users_new, user_gram, boxes, table = step(
        item_factors.T, req.reshape(1, TILE), place, where, weights, user_old
    )
    return users_new, user_gram, mask(table, boxes)


def solution(mesh):
    placed = (
        P("wide", "node"),
        P("wide", None),
        P("wide"),
        P(("wide", "node")),
        P(("wide", "node")),
        P(("wide", "node"), None, None),
        P(("wide", "node"), None),
    )
    return jax.shard_map(
        body,
        mesh=mesh,
        in_specs=placed,
        out_specs=(P(("wide", "node"), None), P(), P("wide", None, "node", None)),
        check_vma=False,
    )
```

```python
import functools

import jax
import jax.numpy as jnp
from jax import lax
from jax.experimental import pallas as pl
from jax.experimental.pallas import tpu as pltpu
from jax.sharding import PartitionSpec as P

TILE = 128
ITERS = 2
NEED = 32
K = 256
QUARTER = 64
RANKS = QUARTER // 2
NB = 64
WIDE = 32
NODE = 4
CORES = 2
PLANE = 16
SIDE = 4
TILES = 64
SHARE = 16
PAIRS = NEED // 2
GROUP = 4
STEPS = PAIRS // GROUP
SPAN = GROUP * 2 * TILE
HALF = 128
BIT = 64
BAND = K // (NODE * CORES)
STRIP = BAND // SIDE
PART = K // PLANE
RIDGE = 1.0
EPS = 1e-06

MESH = pl.DeviceIdType.MESH
F32 = jnp.float32
BF16 = jnp.bfloat16


def split(x):
    high = x.astype(BF16)
    return high, (x - high.astype(F32)).astype(BF16)


def dot(a, b, contract):
    return lax.dot_general(a, b, ((contract[:1], contract[1:]), ((), ())), preferred_element_type=F32)


def dot3(a, b, contract):
    left = jnp.concatenate([a[0], a[0], a[1]], axis=contract[0])
    right = jnp.concatenate([b[0], b[1], b[0]], axis=contract[1])
    return dot(left, right, contract)


def place_at():
    wide, node = lax.axis_index("wide"), lax.axis_index("node")
    return wide, node, wide // CORES, lax.rem(wide, CORES)


def remote(src, dst, send, recv, wide, node):
    return pltpu.make_async_remote_copy(
        src_ref=src, dst_ref=dst, send_sem=send, recv_sem=recv, device_id=(wide, node), device_id_type=MESH
    )


def each(low, high, step):
    lax.fori_loop(low, high, lambda i, c: (step(i), c)[1], 0)


def greet():
    wide, node, spot, core = place_at()
    barrier = pltpu.get_barrier_semaphore()

    def to_wide(k):
        pl.semaphore_signal(barrier, inc=1, device_id=(lax.rem(wide + k, WIDE), node), device_id_type=MESH)

    each(1, WIDE, to_wide)
    for dx in range(1, NODE):
        for dc in range(CORES):
            pl.semaphore_signal(
                barrier,
                inc=1,
                device_id=(spot * CORES + lax.rem(core + dc, CORES), lax.rem(node + dx, NODE)),
                device_id_type=MESH,
            )
    pl.semaphore_wait(barrier, WIDE - 1 + (NODE - 1) * CORES)


class Summer:
    def __init__(self, part, total, red, mid, sems):
        self.part, self.total, self.red, self.mid, self.sems = part, total, red, mid, sems
        self.wide, self.node, self.spot, self.core = place_at()
        self.eighth = self.node * CORES + self.core
        self.rows = pl.ds(pl.multiple_of(self.spot * PART, PART), PART)

    def over_plane(self, k, stage):
        spot = lax.rem(self.spot + k, PLANE)
        send, recv = self.sems.at[stage, 0, k], self.sems.at[stage, 1, k]
        if stage == 0:
            src = self.part.at[pl.ds(pl.multiple_of(spot * PART, PART), PART)]
            dst = self.red.at[self.spot]
        else:
            src = dst = self.total.at[self.rows]
        return remote(src, dst, send, recv, spot * CORES + self.core, self.node)

    def over_eight(self, k):
        other = lax.rem(self.eighth + k, NODE * CORES)
        slot = self.mid.at[self.eighth]
        wide = self.spot * CORES + lax.rem(other, CORES)
        return remote(slot, slot, self.sems.at[1, 0, k], self.sems.at[1, 1, k], wide, other // CORES)

    def first(self):
        each(1, PLANE, lambda k: self.over_plane(k, 0).start())
        self.red[self.spot] = self.part[self.rows, :]

    def second(self):
        each(1, PLANE, lambda k: self.over_plane(k, 0).wait_recv())
        total = self.red[0]
        for i in range(1, PLANE):
            total = total + self.red[i]
        self.mid[self.eighth] = total
        each(1, NODE * CORES, lambda k: self.over_eight(k).start())

    def third(self):
        each(1, NODE * CORES, lambda k: self.over_eight(k).wait_recv())
        total = self.mid[0]
        for i in range(1, NODE * CORES):
            total = total + self.mid[i]
        self.total[self.rows, :] = total
        each(1, PLANE, lambda k: self.over_plane(k, 2).start())

    def last(self):
        each(1, PLANE, lambda k: self.over_plane(k, 2).wait_recv())
        each(1, PLANE, lambda k: self.over_plane(k, 0).wait_send())
        each(1, NODE * CORES, lambda k: self.over_eight(k).wait_send())
        each(1, PLANE, lambda k: self.over_plane(k, 2).wait_send())


class LineSummer:
    def __init__(self, part, total, eight, own, along_y, along_z, sems):
        self.part, self.total, self.eight, self.own = part, total, eight, own
        self.along_y, self.along_z, self.sems = along_y, along_z, sems
        self.wide, self.node, self.spot, self.core = place_at()
        self.y, self.z = self.spot // SIDE, lax.rem(self.spot, SIDE)
        self.eighth = self.node * CORES + self.core

    def rows(self, eighth):
        return pl.ds(pl.multiple_of(eighth * BAND, BAND), BAND)

    def over_eight(self, k, stage):
        other = lax.rem(self.eighth + k, NODE * CORES)
        if stage == 0:
            src, dst = self.part.at[self.rows(other)], self.eight.at[self.eighth]
        else:
            src = dst = self.total.at[self.rows(self.eighth)]
        wide = self.spot * CORES + lax.rem(other, CORES)
        return remote(src, dst, self.sems.at[stage, 0, k], self.sems.at[stage, 1, k], wide, other // CORES)

    def over_y(self, k, stage):
        other = lax.rem(self.y + k, SIDE)
        if stage == 1:
            src, dst = self.own.at[other], self.along_y.at[self.y]
        else:
            src = dst = self.total.at[self.fine()]
        wide = (other * SIDE + self.z) * CORES + self.core
        return remote(src, dst, self.sems.at[stage, 0, k], self.sems.at[stage, 1, k], wide, self.node)

    def over_z(self, k):
        wide = (self.y * SIDE + lax.rem(self.z + k, SIDE)) * CORES + self.core
        slot = self.along_z.at[self.z]
        return remote(slot, slot, self.sems.at[2, 0, k], self.sems.at[2, 1, k], wide, self.node)

    def fine(self):
        return pl.ds(pl.multiple_of(self.eighth * BAND + self.y * STRIP, STRIP), STRIP)

    def first(self):
        each(1, NODE * CORES, lambda k: self.over_eight(k, 0).start())
        self.eight[self.eighth] = self.part[self.rows(self.eighth), :]

    def second(self):
        each(1, NODE * CORES, lambda k: self.over_eight(k, 0).wait_recv())
        for j in range(SIDE):
            rows = slice(j * STRIP, (j + 1) * STRIP)
            total = self.eight[0, rows, :]
            for i in range(1, NODE * CORES):
                total = total + self.eight[i, rows, :]
            self.own[j] = total
        each(1, SIDE, lambda k: self.over_y(k, 1).start())
        self.along_y[self.y] = self.own[self.y]

    def third(self):
        each(1, SIDE, lambda k: self.over_y(k, 1).wait_recv())
        self.along_z[self.z] = (self.along_y[0] + self.along_y[1]) + (self.along_y[2] + self.along_y[3])
        each(1, SIDE, lambda k: self.over_z(k).start())

    def fourth(self):
        each(1, SIDE, lambda k: self.over_z(k).wait_recv())
        total = (self.along_z[0] + self.along_z[1]) + (self.along_z[2] + self.along_z[3])
        self.total[self.fine(), :] = total
        each(1, SIDE, lambda k: self.over_y(k, 3).start())

    def fifth(self):
        each(1, SIDE, lambda k: self.over_y(k, 3).wait_recv())
        each(1, NODE * CORES, lambda k: self.over_eight(k, 4).start())

    def last(self):
        each(1, NODE * CORES, lambda k: self.over_eight(k, 4).wait_recv())
        each(1, NODE * CORES, lambda k: self.over_eight(k, 0).wait_send())
        each(1, SIDE, lambda k: self.over_y(k, 1).wait_send())
        each(1, SIDE, lambda k: self.over_z(k).wait_send())
        each(1, SIDE, lambda k: self.over_y(k, 3).wait_send())
        each(1, NODE * CORES, lambda k: self.over_eight(k, 4).wait_send())


def plan_kernel(owner, slot, index, count, req, place, where, seen):
    def clear(i):
        req[i] = -1
        where[i] = -1

    def clear_rest(i):
        req[i] = -1

    each(0, NB, clear)
    each(NB, TILE, clear_rest)
    each(0, WIDE, lambda i: seen.__setitem__(i, 0))

    def entry(e):
        o = owner[e]
        at = 2 * o + seen[o]
        seen[o] = seen[o] + 1
        place[e] = at
        req[at] = slot[e]

    each(0, NEED, entry)

    def block(b):
        where[index[b]] = b

    each(0, count[0], block)


def plan(owner, slot, index, count):
    smem = pl.BlockSpec(memory_space=pltpu.SMEM)
    return pl.pallas_call(
        plan_kernel,
        out_shape=[
            jax.ShapeDtypeStruct((TILE,), jnp.int32),
            jax.ShapeDtypeStruct((NEED,), jnp.int32),
            jax.ShapeDtypeStruct((NB,), jnp.int32),
        ],
        in_specs=[smem] * 4,
        out_specs=[smem] * 3,
        scratch_shapes=[pltpu.SMEM((WIDE,), jnp.int32)],
        name="plan",
    )(owner, slot, index, count)


def step_kernel(
    item, req, place, where, weights_in, user_in,
    users, user_gram, boxes, table,
    tiles, full, relay, outbox, inbox_low, inbox_high, asked, lists, weights, user, gram, part, red, mid, eight, own_band, along_y, along_z, high, low, dense, spread,
    sum_sems, line_sum_sems, row_sems, ask_sems, tile_sems, ring_sems, line_sems, cross_sems, sib_sems,
    load_sems, bring_sems, own_sems, local_sem,
):
    wide, node, spot, core = place_at()
    inboxes = inbox_low, inbox_high

    def load(t):
        return pltpu.make_async_copy(
            item.at[:, pl.ds(pl.multiple_of(t * TILE, TILE), TILE)], tiles.at[t], load_sems.at[t]
        )

    each(0, TILES, lambda t: load(t).start())
    bring_weights = pltpu.make_async_copy(weights_in, weights, bring_sems.at[0])
    bring_user = pltpu.make_async_copy(user_in, user, bring_sems.at[1])
    bring_weights.start()
    bring_user.start()
    greet()

    def quarter(x):
        return pl.ds(pl.multiple_of(x * QUARTER, QUARTER), QUARTER)

    def share(x):
        return pl.ds(pl.multiple_of(x * SHARE, SHARE), SHARE)

    right, left = lax.rem(node + 1, NODE), lax.rem(node + NODE - 1, NODE)
    across = lax.rem(node + 2, NODE)

    def part_share(x, way):
        return pl.ds(pl.multiple_of(x * SHARE + way * SHARE // 2, SHARE // 2), SHARE // 2)

    def rows_near(way):
        x = (right, left)[way]
        return remote(
            tiles.at[share(x)], full.at[:, quarter(node), :], row_sems.at[0, 0, way], row_sems.at[1, 0, way], wide, x
        )

    def rows_relay(way):
        return remote(
            tiles.at[part_share(across, way)], relay.at[way],
            row_sems.at[0, 1, way], row_sems.at[1, 1, way], wide, (right, left)[way],
        )

    def rows_far(way):
        return remote(
            relay.at[way], full.at[pl.ds(way * SHARE // 2, SHARE // 2), quarter((left, right)[way]), :],
            row_sems.at[0, 2, way], row_sems.at[1, 2, way], wide, (right, left)[way],
        )

    def ask(k):
        return remote(
            req, table.at[wide], ask_sems.at[0, k], ask_sems.at[1, k], lax.rem(wide + k, WIDE), node
        )

    def serve(k, part):
        other = lax.rem(wide + k, WIDE)
        return remote(
            outbox.at[part, other], inboxes[part].at[pl.ds(2 * wide, 2)],
            tile_sems.at[0, part, k], tile_sems.at[1, part, k], other, node,
        )

    each(1, WIDE, lambda k: ask(k).start())
    each(0, TILES, lambda t: load(t).wait())
    for way in range(2):
        rows_relay(way).start()
    for way in range(2):
        rows_near(way).start()
    table[wide] = req[...]
    full[:, quarter(node), :] = tiles[share(node)]
    each(1, WIDE, lambda k: ask(k).wait_recv())
    to_scalars = pltpu.make_async_copy(table, asked, local_sem)
    to_scalars.start()
    to_scalars.wait()

    def fill(k, part):
        other = lax.rem(wide + k, WIDE)
        for r in range(2):
            at = jnp.maximum(asked[other, 0, 2 * wide + r], 0)
            outbox[part, other, r] = tiles[at, part * RANKS : (part + 1) * RANKS, :]
        serve(k, part).start()

    for part_rank in range(2):
        each(1, WIDE, lambda k, part_rank=part_rank: fill(k, part_rank))
    for r in range(2):
        mine = tiles[jnp.maximum(asked[wide, 0, 2 * wide + r], 0)]
        for half in range(2):
            inboxes[half][2 * wide + r] = mine[half * RANKS : (half + 1) * RANKS]
    for way in range(2):
        rows_relay(way).wait_recv()
        rows_far(way).start()

    def pass_on(c, x, way, half):
        stage = 0 if x is node else 1
        ranks = pl.ds(pl.multiple_of(x * QUARTER + half * RANKS, RANKS), RANKS)
        here = lists.at[pl.ds(GROUP * c, GROUP), ranks, :]
        sems = ring_sems.at[half, stage]
        return remote(here, here, sems.at[0, way, c], sems.at[1, way, c], wide, (right, left)[way])

    def pick(c, half):
        ranks = pl.ds(pl.multiple_of(node * QUARTER + half * RANKS, RANKS), RANKS)
        for j in range(GROUP):
            for r in range(2):
                at = place[2 * GROUP * c + 2 * j + r]
                lists[GROUP * c + j, ranks, r * TILE : (r + 1) * TILE] = inboxes[half][at]
        pass_on(c, node, 0, half).start()
        pass_on(c, node, 1, half).start()

    def forward(c, half):
        pass_on(2 * c, node, 0, half).wait_recv()
        pass_on(2 * c, left, 0, half).start()
        pass_on(2 * c + 1, node, 1, half).wait_recv()
        pass_on(2 * c + 1, right, 1, half).start()

    each(1, WIDE, lambda k: serve(k, 0).wait_recv())
    each(0, STEPS, lambda c: pick(c, 0))
    for way in range(2):
        rows_near(way).wait_recv()
        rows_far(way).wait_recv()
    part[...] = jnp.zeros_like(part)

    def multiply(i):
        pair = split(jnp.concatenate([full[4 * i + j] for j in range(4)], axis=1))
        part[...] += dot3(pair, pair, (1, 1))

    each(0, SHARE // 4, multiply)
    summer = Summer(part, gram, red, mid, sum_sems)
    summer.first()

    each(0, STEPS // 2, lambda c: forward(c, 0))
    each(1, WIDE, lambda k: serve(k, 1).wait_recv())
    summer.second()
    each(0, STEPS, lambda c: pick(c, 1))
    each(0, STEPS // 2, lambda c: forward(c, 1))
    summer.third()
    bring_weights.wait()
    bring_user.wait()

    x = user[...]
    pair = split(x)
    spread[...] = jnp.zeros_like(spread)

    def arrive(c, half):
        pass_on(2 * c, node, 1, half).wait_recv()
        pass_on(2 * c + 1, node, 0, half).wait_recv()
        pass_on(2 * c, left, 0, half).wait_recv()
        pass_on(2 * c + 1, right, 1, half).wait_recv()

    each(0, STEPS // 2, lambda c: arrive(c, 0))

    def begin(i):
        parts = [split(lists[GROUP * i + j]) for j in range(GROUP)]
        v = tuple(jnp.concatenate([q[k] for q in parts], axis=1) for k in range(2))
        high[i], low[i] = v
        s = dot3(pair, v, (1, 0))
        rows = []
        for u in range(2):
            cols = []
            for r in range(2 * GROUP):
                at = where[u * NEED + 2 * GROUP * i + r]
                live = (jnp.minimum(at, 0) + 1).astype(F32)
                c = weights[jnp.maximum(at, 0)] * live
                here = slice(u * TILE, (u + 1) * TILE), slice(r * TILE, (r + 1) * TILE)
                dense[i, here[0], here[1]] = c
                cols.append((c + live) - c * s[here])
            rows.append(jnp.concatenate(cols, axis=1))
        spread[...] += dot3(split(jnp.concatenate(rows, axis=0)), v, (1, 1))

    for c in range(STEPS // 2):
        arrive(c, 1)
        each(2 * c, 2 * c + 2, begin)
    summer.last()

    gram_pair = split(gram[...])

    def globally(d, pair):
        return dot3(pair, gram_pair, (1, 0)) + RIDGE * d

    residual = spread[...] - globally(x, pair)
    direction = residual
    norm = jnp.sum(residual * residual, axis=1, keepdims=True)

    pair = split(direction)
    spread[...] = jnp.zeros_like(spread)

    def apply(i):
        v = (high[i], low[i])
        t = dot3(pair, v, (1, 0)) * dense[i]
        spread[...] += dot3(split(t), v, (1, 1))

    each(0, STEPS, apply)
    applied = spread[...] + globally(direction, pair)
    step = norm / (jnp.sum(direction * applied, axis=1, keepdims=True) + EPS)
    x = x + step * direction
    residual = residual - step * applied
    following = jnp.sum(residual * residual, axis=1, keepdims=True)
    direction = residual + following / (norm + EPS) * direction
    norm = following

    pair = split(direction)
    spread[...] = direction * globally(direction, pair)

    def curve(i):
        s = dot3(pair, (high[i], low[i]), (1, 0))
        bend = s * s * dense[i]
        total = spread[...]
        for j in range(GROUP):
            total = total + bend[:, j * 2 * TILE : (j + 1) * 2 * TILE]
        spread[...] = total

    each(0, STEPS, curve)
    step = norm / (jnp.sum(spread[...], axis=1, keepdims=True) + EPS)
    x = x + step * direction
    users[...] = x

    y, z = spot // SIDE, lax.rem(spot, SIDE)
    def turn(a, d):
        return lax.rem(a + (d + SIDE), SIDE)

    def block(dy, dz):
        return (turn(y, dy) * SIDE + turn(z, dz)) * CORES + core

    def neighbour(axis, way):
        d = 1 if way == 0 else -1
        return block(d, 0) if axis == 0 else block(0, d)

    def rows(half, bit):
        if bit is None:
            return pl.ds(half * HALF, HALF)
        return pl.ds(half * HALF + bit * BIT, BIT)

    def line(half, way, far):
        axis = half
        d = 0 if not far else (-1 if way == 0 else 1)
        at = block(d, 0) if axis == 0 else block(0, d)
        r = rows(half, way if far else None)
        src = users.at[r] if not far else boxes.at[at, r]
        return remote(
            src, boxes.at[at, r], line_sems.at[0, half, way, far], line_sems.at[1, half, way, far],
            neighbour(axis, way), node,
        )

    def cross(half, along, way, far):
        axis = 1 - half
        d = 0 if not far else (-1 if way == 0 else 1)
        at = block(along, d) if axis == 1 else block(d, along)
        r = rows(half, way if far else None)
        src = users.at[r] if (not far and along == 0) else boxes.at[at, r]
        return remote(
            src, boxes.at[at, r],
            cross_sems.at[0, half, along % SIDE, way, far], cross_sems.at[1, half, along % SIDE, way, far],
            neighbour(axis, way), node,
        )

    def sibling(half, along, over):
        at = block(along, over) if half == 0 else block(over, along)
        r = rows(half, None)
        src = users.at[r] if (along == 0 and over == 0) else boxes.at[at, r]
        i = (along % SIDE) * SIDE + over % SIDE
        return remote(
            src, boxes.at[at, r], sib_sems.at[0, half, i], sib_sems.at[1, half, i],
            spot * CORES + 1 - core, node,
        )

    own = pltpu.make_async_copy(users, boxes.at[wide], own_sems.at[0])
    own.start()
    for half in range(2):
        for way in range(2):
            line(half, way, 0).start()
    for half in range(2):
        for way in range(2):
            cross(half, 0, way, 0).start()
    for half in range(2):
        sibling(half, 0, 0).start()

    pair = split(x)
    part[...] = dot3(pair, pair, (0, 0))
    summer = LineSummer(part, user_gram, eight, own_band, along_y, along_z, line_sum_sems)
    summer.first()

    def come_from(way):
        return -1 if way == 0 else 1

    for way in range(2):
        for half in range(2):
            line(half, way, 0).wait_recv()
            line(half, way, 1).start()
            for w in range(2):
                cross(half, come_from(way), w, 0).start()
            sibling(half, come_from(way), 0).start()
    summer.second()
    for half in range(2):
        for way in range(2):
            line(half, way, 1).wait_recv()
        for w in range(2):
            cross(half, 2, w, 0).start()
        sibling(half, 2, 0).start()
    summer.third()
    for along in (0, -1, 1, 2):
        for half in range(2):
            for way in range(2):
                cross(half, along, way, 0).wait_recv()
                cross(half, along, way, 1).start()
                sibling(half, along, come_from(way)).start()
        if along == -1:
            summer.fourth()
        if along == 2:
            summer.fifth()
    for along in (0, -1, 1, 2):
        for half in range(2):
            for way in range(2):
                cross(half, along, way, 1).wait_recv()
            sibling(half, along, 2).start()
    summer.last()
    for along in (0, -1, 1, 2):
        for half in range(2):
            for over in (0, -1, 1, 2):
                sibling(half, along, over).wait()
            for way in range(2):
                for far in range(2):
                    cross(half, along, way, far).wait_send()
    for half in range(2):
        for way in range(2):
            for far in range(2):
                line(half, way, far).wait_send()
    own.wait()

    for half in range(2):
        for way in range(2):
            each(0, STEPS, lambda c, half=half, way=way: pass_on(c, node, way, half).wait_send())
        for c in range(STEPS // 2):
            pass_on(2 * c, left, 0, half).wait_send()
            pass_on(2 * c + 1, right, 1, half).wait_send()
    for way in range(2):
        rows_relay(way).wait_send()
        rows_near(way).wait_send()
        rows_far(way).wait_send()
    each(1, WIDE, lambda k: ask(k).wait_send())
    for part_rank in range(2):
        each(1, WIDE, lambda k, part_rank=part_rank: serve(k, part_rank).wait_send())


def step(item, req, place, where, weights, user):
    vmem = pl.BlockSpec(memory_space=pltpu.VMEM)
    smem = pl.BlockSpec(memory_space=pltpu.SMEM)
    hbm = pl.BlockSpec(memory_space=pl.ANY)
    return pl.pallas_call(
        step_kernel,
        out_shape=[
            pltpu.VMEM((K, K), F32),
            pltpu.VMEM((K, K), F32),
            pltpu.VMEM((WIDE, K, K), F32),
            pltpu.VMEM((WIDE, 1, TILE), jnp.int32),
        ],
        in_specs=[hbm, vmem, smem, smem, hbm, hbm],
        out_specs=[vmem] * 4,
        scratch_shapes=[
            pltpu.VMEM((TILES, QUARTER, TILE), F32),
            pltpu.VMEM((SHARE, K, TILE), F32),
            pltpu.VMEM((2, SHARE // 2, QUARTER, TILE), F32),
            pltpu.VMEM((2, WIDE, 2, RANKS, TILE), F32),
            pltpu.VMEM((2 * WIDE, RANKS, TILE), F32),
            pltpu.VMEM((2 * WIDE, RANKS, TILE), F32),
            pltpu.SMEM((WIDE, 1, TILE), jnp.int32),
            pltpu.VMEM((PAIRS, K, 2 * TILE), F32),
            pltpu.VMEM((NB, TILE, TILE), F32),
            pltpu.VMEM((K, K), F32),
            pltpu.VMEM((K, K), F32),
            pltpu.VMEM((K, K), F32),
            pltpu.VMEM((PLANE, PART, K), F32),
            pltpu.VMEM((NODE * CORES, PART, K), F32),
            pltpu.VMEM((NODE * CORES, BAND, K), F32),
            pltpu.VMEM((SIDE, STRIP, K), F32),
            pltpu.VMEM((SIDE, STRIP, K), F32),
            pltpu.VMEM((SIDE, STRIP, K), F32),
            pltpu.VMEM((STEPS, K, SPAN), BF16),
            pltpu.VMEM((STEPS, K, SPAN), BF16),
            pltpu.VMEM((STEPS, K, SPAN), F32),
            pltpu.VMEM((K, K), F32),
            pltpu.SemaphoreType.DMA((3, 2, PLANE)),
            pltpu.SemaphoreType.DMA((5, 2, NODE * CORES)),
            pltpu.SemaphoreType.DMA((2, 3, 2)),
            pltpu.SemaphoreType.DMA((2, WIDE)),
            pltpu.SemaphoreType.DMA((2, 2, WIDE)),
            pltpu.SemaphoreType.DMA((2, 2, 2, 2, STEPS)),
            pltpu.SemaphoreType.DMA((2, 2, 2, 2)),
            pltpu.SemaphoreType.DMA((2, 2, SIDE, 2, 2)),
            pltpu.SemaphoreType.DMA((2, 2, PLANE)),
            pltpu.SemaphoreType.DMA((TILES,)),
            pltpu.SemaphoreType.DMA((2,)),
            pltpu.SemaphoreType.DMA((1,)),
            pltpu.SemaphoreType.DMA,
        ],
        compiler_params=pltpu.CompilerParams(
            collective_id=0, has_side_effects=True, vmem_limit_bytes=50 * 1024 * 1024
        ),
        name="step",
    )(item, req, place, where, weights, user)


def mask_kernel(rows, boxes, users_in, gram_in, users_new, user_gram, out, table, zeros, sems):
    scalars = pltpu.make_async_copy(rows, table, sems.at[WIDE + 2])
    scalars.start()
    users = pltpu.make_async_copy(users_in, users_new, sems.at[WIDE])
    gram = pltpu.make_async_copy(gram_in, user_gram, sems.at[WIDE + 1])
    users.start()
    gram.start()
    wide = lax.axis_index("wide")
    zeros[...] = jnp.zeros_like(zeros)
    scalars.wait()

    def begin(g):
        named = table[g, 0, 2 * wide] >= 0

        @pl.when(named)
        def _():
            pltpu.make_async_copy(boxes.at[g], out.at[0, g], sems.at[g]).start()

        @pl.when(jnp.logical_not(named))
        def _():
            pltpu.make_async_copy(zeros, out.at[0, g], sems.at[g]).start()

    each(0, WIDE, begin)
    each(0, WIDE, lambda g: pltpu.make_async_copy(zeros, out.at[0, g], sems.at[g]).wait())
    users.wait()
    gram.wait()


def mask(table, boxes, users, gram):
    return pl.pallas_call(
        mask_kernel,
        out_shape=[
            jax.ShapeDtypeStruct((K, K), F32),
            jax.ShapeDtypeStruct((K, K), F32),
            jax.ShapeDtypeStruct((1, WIDE, K, K), F32),
        ],
        in_specs=[pl.BlockSpec(memory_space=pltpu.VMEM)] * 4,
        out_specs=[pl.BlockSpec(memory_space=pl.ANY)] * 3,
        scratch_shapes=[
            pltpu.SMEM((WIDE, 1, TILE), jnp.int32),
            pltpu.VMEM((K, K), F32),
            pltpu.SemaphoreType.DMA((WIDE + 3,)),
        ],
        compiler_params=pltpu.CompilerParams(vmem_limit_bytes=10 * 1024 * 1024),
        name="mask",
    )(table, boxes, users, gram)


def body(item_factors, need_owner, need_slot, block_index, block_count, weights, user_old):
    req, place, where = plan(need_owner[:, 0], need_slot, block_index, block_count)
    users_new, user_gram, boxes, table = step(
        item_factors.T, req.reshape(1, TILE), place, where, weights, user_old
    )
    return tuple(mask(table, boxes, users_new, user_gram))


def solution(mesh):
    placed = (
        P("wide", "node"),
        P("wide", None),
        P("wide"),
        P(("wide", "node")),
        P(("wide", "node")),
        P(("wide", "node"), None, None),
        P(("wide", "node"), None),
    )
    return jax.shard_map(
        body,
        mesh=mesh,
        in_specs=placed,
        out_specs=(P(("wide", "node"), None), P(), P("wide", None, "node", None)),
        check_vma=False,
    )
```

```python
import functools

import jax
import jax.numpy as jnp
from jax import lax
from jax.experimental import pallas as pl
from jax.experimental.pallas import tpu as pltpu
from jax.sharding import PartitionSpec as P

TILE = 128
ITERS = 2
NEED = 32
K = 256
QUARTER = 64
RANKS = QUARTER // 2
NB = 64
WIDE = 32
NODE = 4
CORES = 2
PLANE = 16
SIDE = 4
TILES = 64
SHARE = 16
PAIRS = NEED // 2
GROUP = 4
STEPS = PAIRS // GROUP
HALF = 128
BIT = 64
BAND = K // (NODE * CORES)
STRIP = BAND // SIDE
PART = K // PLANE
RIDGE = 1.0
EPS = 1e-06

MESH = pl.DeviceIdType.MESH
F32 = jnp.float32
BF16 = jnp.bfloat16


def split(x):
    high = x.astype(BF16)
    return high, (x - high.astype(F32)).astype(BF16)


def dot(a, b, contract):
    return lax.dot_general(a, b, ((contract[:1], contract[1:]), ((), ())), preferred_element_type=F32)


def dot3(a, b, contract):
    left = jnp.concatenate([a[0], a[0], a[1]], axis=contract[0])
    right = jnp.concatenate([b[0], b[1], b[0]], axis=contract[1])
    return dot(left, right, contract)


def place_at():
    wide, node = lax.axis_index("wide"), lax.axis_index("node")
    return wide, node, wide // CORES, lax.rem(wide, CORES)


def remote(src, dst, send, recv, wide, node):
    return pltpu.make_async_remote_copy(
        src_ref=src, dst_ref=dst, send_sem=send, recv_sem=recv, device_id=(wide, node), device_id_type=MESH
    )


def each(low, high, step):
    lax.fori_loop(low, high, lambda i, c: (step(i), c)[1], 0)


def greet():
    wide, node, spot, core = place_at()
    barrier = pltpu.get_barrier_semaphore()

    def to_wide(k):
        pl.semaphore_signal(barrier, inc=1, device_id=(lax.rem(wide + k, WIDE), node), device_id_type=MESH)

    each(1, WIDE, to_wide)
    for dx in range(1, NODE):
        for dc in range(CORES):
            pl.semaphore_signal(
                barrier,
                inc=1,
                device_id=(spot * CORES + lax.rem(core + dc, CORES), lax.rem(node + dx, NODE)),
                device_id_type=MESH,
            )
    pl.semaphore_wait(barrier, WIDE - 1 + (NODE - 1) * CORES)


class Summer:
    def __init__(self, part, total, red, mid, sems):
        self.part, self.total, self.red, self.mid, self.sems = part, total, red, mid, sems
        self.wide, self.node, self.spot, self.core = place_at()
        self.eighth = self.node * CORES + self.core
        self.rows = pl.ds(pl.multiple_of(self.spot * PART, PART), PART)

    def over_plane(self, k, stage):
        spot = lax.rem(self.spot + k, PLANE)
        send, recv = self.sems.at[stage, 0, k], self.sems.at[stage, 1, k]
        if stage == 0:
            src = self.part.at[pl.ds(pl.multiple_of(spot * PART, PART), PART)]
            dst = self.red.at[self.spot]
        else:
            src = dst = self.total.at[self.rows]
        return remote(src, dst, send, recv, spot * CORES + self.core, self.node)

    def over_eight(self, k):
        other = lax.rem(self.eighth + k, NODE * CORES)
        slot = self.mid.at[self.eighth]
        wide = self.spot * CORES + lax.rem(other, CORES)
        return remote(slot, slot, self.sems.at[1, 0, k], self.sems.at[1, 1, k], wide, other // CORES)

    def first(self):
        each(1, PLANE, lambda k: self.over_plane(k, 0).start())
        self.red[self.spot] = self.part[self.rows, :]

    def second(self):
        each(1, PLANE, lambda k: self.over_plane(k, 0).wait_recv())
        total = self.red[0]
        for i in range(1, PLANE):
            total = total + self.red[i]
        self.mid[self.eighth] = total
        each(1, NODE * CORES, lambda k: self.over_eight(k).start())

    def third(self):
        each(1, NODE * CORES, lambda k: self.over_eight(k).wait_recv())
        total = self.mid[0]
        for i in range(1, NODE * CORES):
            total = total + self.mid[i]
        self.total[self.rows, :] = total
        each(1, PLANE, lambda k: self.over_plane(k, 2).start())

    def last(self):
        each(1, PLANE, lambda k: self.over_plane(k, 2).wait_recv())
        each(1, PLANE, lambda k: self.over_plane(k, 0).wait_send())
        each(1, NODE * CORES, lambda k: self.over_eight(k).wait_send())
        each(1, PLANE, lambda k: self.over_plane(k, 2).wait_send())


class LineSummer:
    def __init__(self, part, total, eight, own, along_y, along_z, sems):
        self.part, self.total, self.eight, self.own = part, total, eight, own
        self.along_y, self.along_z, self.sems = along_y, along_z, sems
        self.wide, self.node, self.spot, self.core = place_at()
        self.y, self.z = self.spot // SIDE, lax.rem(self.spot, SIDE)
        self.eighth = self.node * CORES + self.core

    def rows(self, eighth):
        return pl.ds(pl.multiple_of(eighth * BAND, BAND), BAND)

    def over_eight(self, k, stage):
        other = lax.rem(self.eighth + k, NODE * CORES)
        if stage == 0:
            src, dst = self.part.at[self.rows(other)], self.eight.at[self.eighth]
        else:
            src = dst = self.total.at[self.rows(self.eighth)]
        wide = self.spot * CORES + lax.rem(other, CORES)
        return remote(src, dst, self.sems.at[stage, 0, k], self.sems.at[stage, 1, k], wide, other // CORES)

    def over_y(self, k, stage):
        other = lax.rem(self.y + k, SIDE)
        if stage == 1:
            src, dst = self.own.at[other], self.along_y.at[self.y]
        else:
            src = dst = self.total.at[self.fine()]
        wide = (other * SIDE + self.z) * CORES + self.core
        return remote(src, dst, self.sems.at[stage, 0, k], self.sems.at[stage, 1, k], wide, self.node)

    def over_z(self, k):
        wide = (self.y * SIDE + lax.rem(self.z + k, SIDE)) * CORES + self.core
        slot = self.along_z.at[self.z]
        return remote(slot, slot, self.sems.at[2, 0, k], self.sems.at[2, 1, k], wide, self.node)

    def fine(self):
        return pl.ds(pl.multiple_of(self.eighth * BAND + self.y * STRIP, STRIP), STRIP)

    def first(self):
        each(1, NODE * CORES, lambda k: self.over_eight(k, 0).start())
        self.eight[self.eighth] = self.part[self.rows(self.eighth), :]

    def second(self):
        each(1, NODE * CORES, lambda k: self.over_eight(k, 0).wait_recv())
        for j in range(SIDE):
            rows = slice(j * STRIP, (j + 1) * STRIP)
            total = self.eight[0, rows, :]
            for i in range(1, NODE * CORES):
                total = total + self.eight[i, rows, :]
            self.own[j] = total
        each(1, SIDE, lambda k: self.over_y(k, 1).start())
        self.along_y[self.y] = self.own[self.y]

    def third(self):
        each(1, SIDE, lambda k: self.over_y(k, 1).wait_recv())
        self.along_z[self.z] = (self.along_y[0] + self.along_y[1]) + (self.along_y[2] + self.along_y[3])
        each(1, SIDE, lambda k: self.over_z(k).start())

    def fourth(self):
        each(1, SIDE, lambda k: self.over_z(k).wait_recv())
        total = (self.along_z[0] + self.along_z[1]) + (self.along_z[2] + self.along_z[3])
        self.total[self.fine(), :] = total
        each(1, SIDE, lambda k: self.over_y(k, 3).start())

    def fifth(self):
        each(1, SIDE, lambda k: self.over_y(k, 3).wait_recv())
        each(1, NODE * CORES, lambda k: self.over_eight(k, 4).start())

    def last(self):
        each(1, NODE * CORES, lambda k: self.over_eight(k, 4).wait_recv())
        each(1, NODE * CORES, lambda k: self.over_eight(k, 0).wait_send())
        each(1, SIDE, lambda k: self.over_y(k, 1).wait_send())
        each(1, SIDE, lambda k: self.over_z(k).wait_send())
        each(1, SIDE, lambda k: self.over_y(k, 3).wait_send())
        each(1, NODE * CORES, lambda k: self.over_eight(k, 4).wait_send())


def plan_kernel(owner, slot, index, count, req, place, where, seen):
    for i in range(TILE):
        req[i] = -1
    for i in range(WIDE):
        seen[i] = 0
    for e in range(NEED):
        o = owner[e]
        before = seen[o]
        seen[o] = before + 1
        place[e] = 2 * o + before
        req[2 * o + before] = slot[e]
    live = count[0]
    for b in range(NB):
        where[index[b]] = jnp.where(b < live, b, -1)


def plan(owner, slot, index, count):
    smem = pl.BlockSpec(memory_space=pltpu.SMEM)
    return pl.pallas_call(
        plan_kernel,
        out_shape=[
            jax.ShapeDtypeStruct((TILE,), jnp.int32),
            jax.ShapeDtypeStruct((NEED,), jnp.int32),
            jax.ShapeDtypeStruct((NB,), jnp.int32),
        ],
        in_specs=[smem] * 4,
        out_specs=[smem] * 3,
        scratch_shapes=[pltpu.SMEM((WIDE,), jnp.int32)],
        name="plan",
    )(owner, slot, index, count)


def step_kernel(
    item, req, place, where, weights_in, user_in,
    users, user_gram, boxes, table,
    tiles, full, relay, outbox, inbox_low, inbox_high, asked, lists, weights, user, gram, part, red, mid, eight, own_band, along_y, along_z, high, low, dense,
    sum_sems, line_sum_sems, row_sems, ask_sems, tile_sems, ring_sems, line_sems, cross_sems, sib_sems,
    load_sems, bring_sems, own_sems, local_sem,
):
    wide, node, spot, core = place_at()
    inboxes = inbox_low, inbox_high

    def load(t):
        return pltpu.make_async_copy(
            item.at[:, pl.ds(pl.multiple_of(t * TILE, TILE), TILE)], tiles.at[t], load_sems.at[t]
        )

    each(0, TILES, lambda t: load(t).start())
    bring_weights = pltpu.make_async_copy(weights_in, weights, bring_sems.at[0])
    bring_user = pltpu.make_async_copy(user_in, user, bring_sems.at[1])
    bring_weights.start()
    bring_user.start()
    greet()

    def quarter(x):
        return pl.ds(pl.multiple_of(x * QUARTER, QUARTER), QUARTER)

    def share(x):
        return pl.ds(pl.multiple_of(x * SHARE, SHARE), SHARE)

    right, left = lax.rem(node + 1, NODE), lax.rem(node + NODE - 1, NODE)
    across = lax.rem(node + 2, NODE)

    def part_share(x, way):
        return pl.ds(pl.multiple_of(x * SHARE + way * SHARE // 2, SHARE // 2), SHARE // 2)

    def rows_near(way):
        x = (right, left)[way]
        return remote(
            tiles.at[share(x)], full.at[:, quarter(node), :], row_sems.at[0, 0, way], row_sems.at[1, 0, way], wide, x
        )

    def rows_relay(way):
        return remote(
            tiles.at[part_share(across, way)], relay.at[way],
            row_sems.at[0, 1, way], row_sems.at[1, 1, way], wide, (right, left)[way],
        )

    def rows_far(way):
        return remote(
            relay.at[way], full.at[pl.ds(way * SHARE // 2, SHARE // 2), quarter((left, right)[way]), :],
            row_sems.at[0, 2, way], row_sems.at[1, 2, way], wide, (right, left)[way],
        )

    def ask(k):
        return remote(
            req, table.at[wide], ask_sems.at[0, k], ask_sems.at[1, k], lax.rem(wide + k, WIDE), node
        )

    def serve(k, part):
        other = lax.rem(wide + k, WIDE)
        return remote(
            outbox.at[part, other], inboxes[part].at[pl.ds(2 * wide, 2)],
            tile_sems.at[0, part, k], tile_sems.at[1, part, k], other, node,
        )

    each(1, WIDE, lambda k: ask(k).start())
    each(0, TILES, lambda t: load(t).wait())
    for way in range(2):
        rows_relay(way).start()
    for way in range(2):
        rows_near(way).start()
    table[wide] = req[...]
    full[:, quarter(node), :] = tiles[share(node)]
    each(1, WIDE, lambda k: ask(k).wait_recv())
    to_scalars = pltpu.make_async_copy(table, asked, local_sem)
    to_scalars.start()
    to_scalars.wait()

    def fill(k, part):
        other = lax.rem(wide + k, WIDE)
        for r in range(2):
            at = jnp.maximum(asked[other, 0, 2 * wide + r], 0)
            outbox[part, other, r] = tiles[at, part * RANKS : (part + 1) * RANKS, :]
        serve(k, part).start()

    for part_rank in range(2):
        each(1, WIDE, lambda k, part_rank=part_rank: fill(k, part_rank))
    for r in range(2):
        mine = tiles[jnp.maximum(asked[wide, 0, 2 * wide + r], 0)]
        for half in range(2):
            inboxes[half][2 * wide + r] = mine[half * RANKS : (half + 1) * RANKS]
    for way in range(2):
        rows_relay(way).wait_recv()
        rows_far(way).start()

    def pass_on(c, x, way, half):
        stage = 0 if x is node else 1
        ranks = pl.ds(pl.multiple_of(x * QUARTER + half * RANKS, RANKS), RANKS)
        here = lists.at[pl.ds(GROUP * c, GROUP), ranks, :]
        sems = ring_sems.at[half, stage]
        return remote(here, here, sems.at[0, way, c], sems.at[1, way, c], wide, (right, left)[way])

    def pick(c, half):
        ranks = pl.ds(pl.multiple_of(node * QUARTER + half * RANKS, RANKS), RANKS)
        for j in range(GROUP):
            for r in range(2):
                at = place[2 * GROUP * c + 2 * j + r]
                lists[GROUP * c + j, ranks, r * TILE : (r + 1) * TILE] = inboxes[half][at]
        pass_on(c, node, 0, half).start()
        pass_on(c, node, 1, half).start()

    def forward(c, half):
        pass_on(2 * c, node, 0, half).wait_recv()
        pass_on(2 * c, left, 0, half).start()
        pass_on(2 * c + 1, node, 1, half).wait_recv()
        pass_on(2 * c + 1, right, 1, half).start()

    each(1, WIDE, lambda k: serve(k, 0).wait_recv())
    each(0, STEPS, lambda c: pick(c, 0))
    for way in range(2):
        rows_near(way).wait_recv()
        rows_far(way).wait_recv()
    part[...] = jnp.zeros_like(part)

    def multiply(i):
        pair = split(jnp.concatenate([full[4 * i + j] for j in range(4)], axis=1))
        part[...] += dot3(pair, pair, (1, 1))

    each(0, SHARE // 4, multiply)
    summer = Summer(part, gram, red, mid, sum_sems)
    summer.first()

    each(0, STEPS // 2, lambda c: forward(c, 0))
    each(1, WIDE, lambda k: serve(k, 1).wait_recv())
    summer.second()
    each(0, STEPS, lambda c: pick(c, 1))
    each(0, STEPS // 2, lambda c: forward(c, 1))
    summer.third()
    bring_weights.wait()
    bring_user.wait()

    x = user[...]
    pair = split(x)

    def arrive(c, half):
        pass_on(2 * c, node, 1, half).wait_recv()
        pass_on(2 * c + 1, node, 0, half).wait_recv()
        pass_on(2 * c, left, 0, half).wait_recv()
        pass_on(2 * c + 1, right, 1, half).wait_recv()

    each(0, STEPS // 2, lambda c: arrive(c, 0))

    def begin(p, total):
        v = split(lists[p])
        high[p], low[p] = v
        s = dot3(pair, v, (1, 0))
        rows = []
        for u in range(2):
            cols = []
            for r in range(2):
                at = where[u * NEED + 2 * p + r]
                live = (jnp.minimum(at, 0) + 1).astype(F32)
                c = weights[jnp.maximum(at, 0)] * live
                here = slice(u * TILE, (u + 1) * TILE), slice(r * TILE, (r + 1) * TILE)
                dense[p, here[0], here[1]] = c
                cols.append((c + live) - c * s[here])
            rows.append(jnp.concatenate(cols, axis=1))
        return total + dot3(split(jnp.concatenate(rows, axis=0)), v, (1, 1))

    total = jnp.zeros((K, K), F32)
    for c in range(STEPS // 2):
        arrive(c, 1)
        for p in range(c * PAIRS // 2, (c + 1) * PAIRS // 2):
            total = begin(p, total)
    summer.last()

    gram_pair = split(gram[...])

    def globally(d, pair):
        return dot3(pair, gram_pair, (1, 0)) + RIDGE * d

    residual = total - globally(x, pair)
    direction = residual
    norm = jnp.sum(residual * residual, axis=1, keepdims=True)

    pair = split(direction)

    def scores(p):
        return dot3(pair, (high[p], low[p]), (1, 0))

    applied = globally(direction, pair)
    s = scores(0)
    for p in range(PAIRS):
        following = scores(p + 1) if p + 1 < PAIRS else None
        applied = applied + dot3(split(s * dense[p]), (high[p], low[p]), (1, 1))
        s = following
    step = norm / (jnp.sum(direction * applied, axis=1, keepdims=True) + EPS)
    x = x + step * direction
    residual = residual - step * applied
    following = jnp.sum(residual * residual, axis=1, keepdims=True)
    direction = residual + following / (norm + EPS) * direction
    norm = following

    pair = split(direction)
    bend = direction * globally(direction, pair)
    for p in range(PAIRS):
        s = scores(p)
        bend = bend + s * s * dense[p]
    step = norm / (jnp.sum(bend, axis=1, keepdims=True) + EPS)
    x = x + step * direction
    users[...] = x

    y, z = spot // SIDE, lax.rem(spot, SIDE)
    def turn(a, d):
        return lax.rem(a + (d + SIDE), SIDE)

    def block(dy, dz):
        return (turn(y, dy) * SIDE + turn(z, dz)) * CORES + core

    def neighbour(axis, way):
        d = 1 if way == 0 else -1
        return block(d, 0) if axis == 0 else block(0, d)

    def rows(half, bit):
        if bit is None:
            return pl.ds(half * HALF, HALF)
        return pl.ds(half * HALF + bit * BIT, BIT)

    def line(half, way, far):
        axis = half
        d = 0 if not far else (-1 if way == 0 else 1)
        at = block(d, 0) if axis == 0 else block(0, d)
        r = rows(half, way if far else None)
        src = users.at[r] if not far else boxes.at[at, r]
        return remote(
            src, boxes.at[at, r], line_sems.at[0, half, way, far], line_sems.at[1, half, way, far],
            neighbour(axis, way), node,
        )

    def cross(half, along, way, far):
        axis = 1 - half
        d = 0 if not far else (-1 if way == 0 else 1)
        at = block(along, d) if axis == 1 else block(d, along)
        r = rows(half, way if far else None)
        src = users.at[r] if (not far and along == 0) else boxes.at[at, r]
        return remote(
            src, boxes.at[at, r],
            cross_sems.at[0, half, along % SIDE, way, far], cross_sems.at[1, half, along % SIDE, way, far],
            neighbour(axis, way), node,
        )

    def sibling(half, along, over):
        at = block(along, over) if half == 0 else block(over, along)
        r = rows(half, None)
        src = users.at[r] if (along == 0 and over == 0) else boxes.at[at, r]
        i = (along % SIDE) * SIDE + over % SIDE
        return remote(
            src, boxes.at[at, r], sib_sems.at[0, half, i], sib_sems.at[1, half, i],
            spot * CORES + 1 - core, node,
        )

    own = pltpu.make_async_copy(users, boxes.at[wide], own_sems.at[0])
    own.start()
    for half in range(2):
        for way in range(2):
            line(half, way, 0).start()
    for half in range(2):
        for way in range(2):
            cross(half, 0, way, 0).start()
    for half in range(2):
        sibling(half, 0, 0).start()

    pair = split(x)
    part[...] = dot3(pair, pair, (0, 0))
    summer = LineSummer(part, user_gram, eight, own_band, along_y, along_z, line_sum_sems)
    summer.first()

    def come_from(way):
        return -1 if way == 0 else 1

    for way in range(2):
        for half in range(2):
            line(half, way, 0).wait_recv()
            line(half, way, 1).start()
            for w in range(2):
                cross(half, come_from(way), w, 0).start()
            sibling(half, come_from(way), 0).start()
    summer.second()
    for half in range(2):
        for way in range(2):
            line(half, way, 1).wait_recv()
        for w in range(2):
            cross(half, 2, w, 0).start()
        sibling(half, 2, 0).start()
    summer.third()
    for along in (0, -1, 1, 2):
        for half in range(2):
            for way in range(2):
                cross(half, along, way, 0).wait_recv()
                cross(half, along, way, 1).start()
                sibling(half, along, come_from(way)).start()
        if along == -1:
            summer.fourth()
        if along == 2:
            summer.fifth()
    for along in (0, -1, 1, 2):
        for half in range(2):
            for way in range(2):
                cross(half, along, way, 1).wait_recv()
            sibling(half, along, 2).start()
    summer.last()
    for along in (0, -1, 1, 2):
        for half in range(2):
            for over in (0, -1, 1, 2):
                sibling(half, along, over).wait()
            for way in range(2):
                for far in range(2):
                    cross(half, along, way, far).wait_send()
    for half in range(2):
        for way in range(2):
            for far in range(2):
                line(half, way, far).wait_send()
    own.wait()

    for half in range(2):
        for way in range(2):
            each(0, STEPS, lambda c, half=half, way=way: pass_on(c, node, way, half).wait_send())
        for c in range(STEPS // 2):
            pass_on(2 * c, left, 0, half).wait_send()
            pass_on(2 * c + 1, right, 1, half).wait_send()
    for way in range(2):
        rows_relay(way).wait_send()
        rows_near(way).wait_send()
        rows_far(way).wait_send()
    each(1, WIDE, lambda k: ask(k).wait_send())
    for part_rank in range(2):
        each(1, WIDE, lambda k, part_rank=part_rank: serve(k, part_rank).wait_send())


def step(item, req, place, where, weights, user):
    vmem = pl.BlockSpec(memory_space=pltpu.VMEM)
    smem = pl.BlockSpec(memory_space=pltpu.SMEM)
    hbm = pl.BlockSpec(memory_space=pl.ANY)
    return pl.pallas_call(
        step_kernel,
        out_shape=[
            pltpu.VMEM((K, K), F32),
            pltpu.VMEM((K, K), F32),
            pltpu.VMEM((WIDE, K, K), F32),
            pltpu.VMEM((WIDE, 1, TILE), jnp.int32),
        ],
        in_specs=[hbm, vmem, smem, smem, hbm, hbm],
        out_specs=[vmem] * 4,
        scratch_shapes=[
            pltpu.VMEM((TILES, QUARTER, TILE), F32),
            pltpu.VMEM((SHARE, K, TILE), F32),
            pltpu.VMEM((2, SHARE // 2, QUARTER, TILE), F32),
            pltpu.VMEM((2, WIDE, 2, RANKS, TILE), F32),
            pltpu.VMEM((2 * WIDE, RANKS, TILE), F32),
            pltpu.VMEM((2 * WIDE, RANKS, TILE), F32),
            pltpu.SMEM((WIDE, 1, TILE), jnp.int32),
            pltpu.VMEM((PAIRS, K, 2 * TILE), F32),
            pltpu.VMEM((NB, TILE, TILE), F32),
            pltpu.VMEM((K, K), F32),
            pltpu.VMEM((K, K), F32),
            pltpu.VMEM((K, K), F32),
            pltpu.VMEM((PLANE, PART, K), F32),
            pltpu.VMEM((NODE * CORES, PART, K), F32),
            pltpu.VMEM((NODE * CORES, BAND, K), F32),
            pltpu.VMEM((SIDE, STRIP, K), F32),
            pltpu.VMEM((SIDE, STRIP, K), F32),
            pltpu.VMEM((SIDE, STRIP, K), F32),
            pltpu.VMEM((PAIRS, K, 2 * TILE), BF16),
            pltpu.VMEM((PAIRS, K, 2 * TILE), BF16),
            pltpu.VMEM((PAIRS, K, 2 * TILE), F32),
            pltpu.SemaphoreType.DMA((3, 2, PLANE)),
            pltpu.SemaphoreType.DMA((5, 2, NODE * CORES)),
            pltpu.SemaphoreType.DMA((2, 3, 2)),
            pltpu.SemaphoreType.DMA((2, WIDE)),
            pltpu.SemaphoreType.DMA((2, 2, WIDE)),
            pltpu.SemaphoreType.DMA((2, 2, 2, 2, STEPS)),
            pltpu.SemaphoreType.DMA((2, 2, 2, 2)),
            pltpu.SemaphoreType.DMA((2, 2, SIDE, 2, 2)),
            pltpu.SemaphoreType.DMA((2, 2, PLANE)),
            pltpu.SemaphoreType.DMA((TILES,)),
            pltpu.SemaphoreType.DMA((2,)),
            pltpu.SemaphoreType.DMA((1,)),
            pltpu.SemaphoreType.DMA,
        ],
        compiler_params=pltpu.CompilerParams(
            collective_id=0, has_side_effects=True, vmem_limit_bytes=50 * 1024 * 1024
        ),
        name="step",
    )(item, req, place, where, weights, user)


def mask_kernel(rows, boxes, users_in, gram_in, users_new, user_gram, out, table, zeros, sems):
    scalars = pltpu.make_async_copy(rows, table, sems.at[WIDE + 2])
    scalars.start()
    users = pltpu.make_async_copy(users_in, users_new, sems.at[WIDE])
    gram = pltpu.make_async_copy(gram_in, user_gram, sems.at[WIDE + 1])
    users.start()
    gram.start()
    wide = lax.axis_index("wide")
    zeros[...] = jnp.zeros_like(zeros)
    scalars.wait()

    def begin(g):
        named = table[g, 0, 2 * wide] >= 0

        @pl.when(named)
        def _():
            pltpu.make_async_copy(boxes.at[g], out.at[0, g], sems.at[g]).start()

        @pl.when(jnp.logical_not(named))
        def _():
            pltpu.make_async_copy(zeros, out.at[0, g], sems.at[g]).start()

    each(0, WIDE, begin)
    each(0, WIDE, lambda g: pltpu.make_async_copy(zeros, out.at[0, g], sems.at[g]).wait())
    users.wait()
    gram.wait()


def mask(table, boxes, users, gram):
    return pl.pallas_call(
        mask_kernel,
        out_shape=[
            jax.ShapeDtypeStruct((K, K), F32),
            jax.ShapeDtypeStruct((K, K), F32),
            jax.ShapeDtypeStruct((1, WIDE, K, K), F32),
        ],
        in_specs=[pl.BlockSpec(memory_space=pltpu.VMEM)] * 4,
        out_specs=[pl.BlockSpec(memory_space=pl.ANY)] * 3,
        scratch_shapes=[
            pltpu.SMEM((WIDE, 1, TILE), jnp.int32),
            pltpu.VMEM((K, K), F32),
            pltpu.SemaphoreType.DMA((WIDE + 3,)),
        ],
        compiler_params=pltpu.CompilerParams(vmem_limit_bytes=10 * 1024 * 1024),
        name="mask",
    )(table, boxes, users, gram)


def body(item_factors, need_owner, need_slot, block_index, block_count, weights, user_old):
    req, place, where = plan(need_owner[:, 0], need_slot, block_index, block_count)
    users_new, user_gram, boxes, table = step(
        item_factors.T, req.reshape(1, TILE), place, where, weights, user_old
    )
    return tuple(mask(table, boxes, users_new, user_gram))


def solution(mesh):
    placed = (
        P("wide", "node"),
        P("wide", None),
        P("wide"),
        P(("wide", "node")),
        P(("wide", "node")),
        P(("wide", "node"), None, None),
        P(("wide", "node"), None),
    )
    return jax.shard_map(
        body,
        mesh=mesh,
        in_specs=placed,
        out_specs=(P(("wide", "node"), None), P(), P("wide", None, "node", None)),
        check_vma=False,
    )
```

```python
import functools

import jax
import jax.numpy as jnp
from jax import lax
from jax.experimental import pallas as pl
from jax.experimental.pallas import tpu as pltpu
from jax.sharding import PartitionSpec as P

TILE = 128
ITERS = 2
NEED = 32
K = 256
QUARTER = 64
RANKS = QUARTER // 2
NB = 64
WIDE = 32
NODE = 4
CORES = 2
PLANE = 16
SIDE = 4
TILES = 64
SHARE = 16
PAIRS = NEED // 2
GROUP = 4
STEPS = PAIRS // GROUP
HALF = 128
BIT = 64
BAND = K // (NODE * CORES)
PART = K // PLANE
RIDGE = 1.0
EPS = 1e-06

MESH = pl.DeviceIdType.MESH
F32 = jnp.float32
BF16 = jnp.bfloat16


def split(x):
    high = x.astype(BF16)
    return high, (x - high.astype(F32)).astype(BF16)


def dot(a, b, contract):
    return lax.dot_general(a, b, ((contract[:1], contract[1:]), ((), ())), preferred_element_type=F32)


def dot3(a, b, contract):
    left = jnp.concatenate([a[0], a[0], a[1]], axis=contract[0])
    right = jnp.concatenate([b[0], b[1], b[0]], axis=contract[1])
    return dot(left, right, contract)


def place_at():
    wide, node = lax.axis_index("wide"), lax.axis_index("node")
    return wide, node, wide // CORES, lax.rem(wide, CORES)


def remote(src, dst, send, recv, wide, node):
    return pltpu.make_async_remote_copy(
        src_ref=src, dst_ref=dst, send_sem=send, recv_sem=recv, device_id=(wide, node), device_id_type=MESH
    )


def each(low, high, step):
    lax.fori_loop(low, high, lambda i, c: (step(i), c)[1], 0)


def greet():
    wide, node, spot, core = place_at()
    barrier = pltpu.get_barrier_semaphore()

    def to_wide(k):
        pl.semaphore_signal(barrier, inc=1, device_id=(lax.rem(wide + k, WIDE), node), device_id_type=MESH)

    each(1, WIDE, to_wide)
    for dx in range(1, NODE):
        for dc in range(CORES):
            pl.semaphore_signal(
                barrier,
                inc=1,
                device_id=(spot * CORES + lax.rem(core + dc, CORES), lax.rem(node + dx, NODE)),
                device_id_type=MESH,
            )
    pl.semaphore_wait(barrier, WIDE - 1 + (NODE - 1) * CORES)


class Summer:
    def __init__(self, part, total, red, mid, sems):
        self.part, self.total, self.red, self.mid, self.sems = part, total, red, mid, sems
        self.wide, self.node, self.spot, self.core = place_at()
        self.eighth = self.node * CORES + self.core
        self.rows = pl.ds(pl.multiple_of(self.spot * PART, PART), PART)

    def over_plane(self, k, stage):
        spot = lax.rem(self.spot + k, PLANE)
        send, recv = self.sems.at[stage, 0, k], self.sems.at[stage, 1, k]
        if stage == 0:
            src = self.part.at[pl.ds(pl.multiple_of(spot * PART, PART), PART)]
            dst = self.red.at[self.spot]
        else:
            src = dst = self.total.at[self.rows]
        return remote(src, dst, send, recv, spot * CORES + self.core, self.node)

    def over_eight(self, k):
        other = lax.rem(self.eighth + k, NODE * CORES)
        slot = self.mid.at[self.eighth]
        wide = self.spot * CORES + lax.rem(other, CORES)
        return remote(slot, slot, self.sems.at[1, 0, k], self.sems.at[1, 1, k], wide, other // CORES)

    def first(self):
        each(1, PLANE, lambda k: self.over_plane(k, 0).start())
        self.red[self.spot] = self.part[self.rows, :]

    def second(self):
        each(1, PLANE, lambda k: self.over_plane(k, 0).wait_recv())
        total = self.red[0]
        for i in range(1, PLANE):
            total = total + self.red[i]
        self.mid[self.eighth] = total
        each(1, NODE * CORES, lambda k: self.over_eight(k).start())

    def third(self):
        each(1, NODE * CORES, lambda k: self.over_eight(k).wait_recv())
        total = self.mid[0]
        for i in range(1, NODE * CORES):
            total = total + self.mid[i]
        self.total[self.rows, :] = total
        each(1, PLANE, lambda k: self.over_plane(k, 2).start())

    def last(self):
        each(1, PLANE, lambda k: self.over_plane(k, 2).wait_recv())
        each(1, PLANE, lambda k: self.over_plane(k, 0).wait_send())
        each(1, NODE * CORES, lambda k: self.over_eight(k).wait_send())
        each(1, PLANE, lambda k: self.over_plane(k, 2).wait_send())


class LineSummer:
    def __init__(self, part, total, eight, along_y, along_z, sems):
        self.part, self.total, self.eight = part, total, eight
        self.along_y, self.along_z, self.sems = along_y, along_z, sems
        self.wide, self.node, self.spot, self.core = place_at()
        self.y, self.z = self.spot // SIDE, lax.rem(self.spot, SIDE)
        self.eighth = self.node * CORES + self.core

    def rows(self, eighth):
        return pl.ds(pl.multiple_of(eighth * BAND, BAND), BAND)

    def over_eight(self, k, stage):
        other = lax.rem(self.eighth + k, NODE * CORES)
        if stage == 0:
            src, dst = self.part.at[self.rows(other)], self.eight.at[self.eighth]
        else:
            src = dst = self.total.at[self.rows(self.eighth)]
        wide = self.spot * CORES + lax.rem(other, CORES)
        return remote(src, dst, self.sems.at[stage, 0, k], self.sems.at[stage, 1, k], wide, other // CORES)

    def over_y(self, k):
        wide = (lax.rem(self.y + k, SIDE) * SIDE + self.z) * CORES + self.core
        slot = self.along_y.at[self.y]
        return remote(slot, slot, self.sems.at[1, 0, k], self.sems.at[1, 1, k], wide, self.node)

    def over_z(self, k):
        wide = (self.y * SIDE + lax.rem(self.z + k, SIDE)) * CORES + self.core
        slot = self.along_z.at[self.z]
        return remote(slot, slot, self.sems.at[2, 0, k], self.sems.at[2, 1, k], wide, self.node)

    def first(self):
        each(1, NODE * CORES, lambda k: self.over_eight(k, 0).start())
        self.eight[self.eighth] = self.part[self.rows(self.eighth), :]

    def second(self):
        each(1, NODE * CORES, lambda k: self.over_eight(k, 0).wait_recv())
        total = self.eight[0]
        for i in range(1, NODE * CORES):
            total = total + self.eight[i]
        self.along_y[self.y] = total
        each(1, SIDE, lambda k: self.over_y(k).start())

    def third(self):
        each(1, SIDE, lambda k: self.over_y(k).wait_recv())
        self.along_z[self.z] = (self.along_y[0] + self.along_y[1]) + (self.along_y[2] + self.along_y[3])
        each(1, SIDE, lambda k: self.over_z(k).start())

    def fourth(self):
        each(1, SIDE, lambda k: self.over_z(k).wait_recv())
        total = (self.along_z[0] + self.along_z[1]) + (self.along_z[2] + self.along_z[3])
        self.total[self.rows(self.eighth), :] = total
        each(1, NODE * CORES, lambda k: self.over_eight(k, 3).start())

    def last(self):
        each(1, NODE * CORES, lambda k: self.over_eight(k, 3).wait_recv())
        each(1, NODE * CORES, lambda k: self.over_eight(k, 0).wait_send())
        each(1, SIDE, lambda k: self.over_y(k).wait_send())
        each(1, SIDE, lambda k: self.over_z(k).wait_send())
        each(1, NODE * CORES, lambda k: self.over_eight(k, 3).wait_send())


def plan_kernel(owner, slot, index, count, req, place, where, seen):
    for i in range(TILE):
        req[i] = -1
    for i in range(WIDE):
        seen[i] = 0
    for e in range(NEED):
        o = owner[e]
        before = seen[o]
        seen[o] = before + 1
        place[e] = 2 * o + before
        req[2 * o + before] = slot[e]
    live = count[0]
    for b in range(NB):
        where[index[b]] = jnp.where(b < live, b, -1)


def plan(owner, slot, index, count):
    smem = pl.BlockSpec(memory_space=pltpu.SMEM)
    return pl.pallas_call(
        plan_kernel,
        out_shape=[
            jax.ShapeDtypeStruct((TILE,), jnp.int32),
            jax.ShapeDtypeStruct((NEED,), jnp.int32),
            jax.ShapeDtypeStruct((NB,), jnp.int32),
        ],
        in_specs=[smem] * 4,
        out_specs=[smem] * 3,
        scratch_shapes=[pltpu.SMEM((WIDE,), jnp.int32)],
        name="plan",
    )(owner, slot, index, count)


def step_kernel(
    item, req, place, where, weights_in, user_in,
    users, user_gram, boxes, table,
    tiles, full, relay, outbox, inbox_low, inbox_high, asked, lists, weights, user, gram, part, red, mid, eight, along_y, along_z, high, low, dense,
    sum_sems, line_sum_sems, row_sems, ask_sems, tile_sems, ring_sems, line_sems, cross_sems, sib_sems,
    load_sems, bring_sems, own_sems, local_sem,
):
    wide, node, spot, core = place_at()
    inboxes = inbox_low, inbox_high

    def load(t):
        return pltpu.make_async_copy(
            item.at[:, pl.ds(pl.multiple_of(t * TILE, TILE), TILE)], tiles.at[t], load_sems.at[t]
        )

    each(0, TILES, lambda t: load(t).start())
    bring_weights = pltpu.make_async_copy(weights_in, weights, bring_sems.at[0])
    bring_user = pltpu.make_async_copy(user_in, user, bring_sems.at[1])
    bring_weights.start()
    bring_user.start()
    greet()

    def quarter(x):
        return pl.ds(pl.multiple_of(x * QUARTER, QUARTER), QUARTER)

    def share(x):
        return pl.ds(pl.multiple_of(x * SHARE, SHARE), SHARE)

    right, left = lax.rem(node + 1, NODE), lax.rem(node + NODE - 1, NODE)
    across = lax.rem(node + 2, NODE)

    def part_share(x, way):
        return pl.ds(pl.multiple_of(x * SHARE + way * SHARE // 2, SHARE // 2), SHARE // 2)

    def rows_near(way):
        x = (right, left)[way]
        return remote(
            tiles.at[share(x)], full.at[:, quarter(node), :], row_sems.at[0, 0, way], row_sems.at[1, 0, way], wide, x
        )

    def rows_relay(way):
        return remote(
            tiles.at[part_share(across, way)], relay.at[way],
            row_sems.at[0, 1, way], row_sems.at[1, 1, way], wide, (right, left)[way],
        )

    def rows_far(way):
        return remote(
            relay.at[way], full.at[pl.ds(way * SHARE // 2, SHARE // 2), quarter((left, right)[way]), :],
            row_sems.at[0, 2, way], row_sems.at[1, 2, way], wide, (right, left)[way],
        )

    def ask(k):
        return remote(
            req, table.at[wide], ask_sems.at[0, k], ask_sems.at[1, k], lax.rem(wide + k, WIDE), node
        )

    def serve(k, part):
        other = lax.rem(wide + k, WIDE)
        return remote(
            outbox.at[part, other], inboxes[part].at[pl.ds(2 * wide, 2)],
            tile_sems.at[0, part, k], tile_sems.at[1, part, k], other, node,
        )

    each(1, WIDE, lambda k: ask(k).start())
    each(0, TILES, lambda t: load(t).wait())
    for way in range(2):
        rows_relay(way).start()
    for way in range(2):
        rows_near(way).start()
    table[wide] = req[...]
    full[:, quarter(node), :] = tiles[share(node)]
    each(1, WIDE, lambda k: ask(k).wait_recv())
    to_scalars = pltpu.make_async_copy(table, asked, local_sem)
    to_scalars.start()
    to_scalars.wait()

    def fill(k, part):
        other = lax.rem(wide + k, WIDE)
        for r in range(2):
            at = jnp.maximum(asked[other, 0, 2 * wide + r], 0)
            outbox[part, other, r] = tiles[at, part * RANKS : (part + 1) * RANKS, :]
        serve(k, part).start()

    for part_rank in range(2):
        each(1, WIDE, lambda k, part_rank=part_rank: fill(k, part_rank))
    for r in range(2):
        mine = tiles[jnp.maximum(asked[wide, 0, 2 * wide + r], 0)]
        for half in range(2):
            inboxes[half][2 * wide + r] = mine[half * RANKS : (half + 1) * RANKS]
    for way in range(2):
        rows_relay(way).wait_recv()
        rows_far(way).start()

    def pass_on(c, x, way, half):
        stage = 0 if x is node else 1
        ranks = pl.ds(pl.multiple_of(x * QUARTER + half * RANKS, RANKS), RANKS)
        here = lists.at[pl.ds(GROUP * c, GROUP), ranks, :]
        sems = ring_sems.at[half, stage]
        return remote(here, here, sems.at[0, way, c], sems.at[1, way, c], wide, (right, left)[way])

    def pick(c, half):
        ranks = pl.ds(pl.multiple_of(node * QUARTER + half * RANKS, RANKS), RANKS)
        for j in range(GROUP):
            for r in range(2):
                at = place[2 * GROUP * c + 2 * j + r]
                lists[GROUP * c + j, ranks, r * TILE : (r + 1) * TILE] = inboxes[half][at]
        pass_on(c, node, 0, half).start()
        pass_on(c, node, 1, half).start()

    def forward(c, half):
        pass_on(2 * c, node, 0, half).wait_recv()
        pass_on(2 * c, left, 0, half).start()
        pass_on(2 * c + 1, node, 1, half).wait_recv()
        pass_on(2 * c + 1, right, 1, half).start()

    each(1, WIDE, lambda k: serve(k, 0).wait_recv())
    each(0, STEPS, lambda c: pick(c, 0))
    for way in range(2):
        rows_near(way).wait_recv()
        rows_far(way).wait_recv()
    part[...] = jnp.zeros_like(part)

    def multiply(i):
        pair = split(jnp.concatenate([full[4 * i + j] for j in range(4)], axis=1))
        part[...] += dot3(pair, pair, (1, 1))

    each(0, SHARE // 4, multiply)
    summer = Summer(part, gram, red, mid, sum_sems)
    summer.first()

    each(0, STEPS // 2, lambda c: forward(c, 0))
    each(1, WIDE, lambda k: serve(k, 1).wait_recv())
    summer.second()
    each(0, STEPS, lambda c: pick(c, 1))
    each(0, STEPS // 2, lambda c: forward(c, 1))
    summer.third()
    bring_weights.wait()
    bring_user.wait()

    x = user[...]
    pair = split(x)

    def arrive(c, half):
        pass_on(2 * c, node, 1, half).wait_recv()
        pass_on(2 * c + 1, node, 0, half).wait_recv()
        pass_on(2 * c, left, 0, half).wait_recv()
        pass_on(2 * c + 1, right, 1, half).wait_recv()

    each(0, STEPS // 2, lambda c: arrive(c, 0))

    def begin(p, total):
        v = split(lists[p])
        high[p], low[p] = v
        s = dot3(pair, v, (1, 0))
        rows = []
        for u in range(2):
            cols = []
            for r in range(2):
                at = where[u * NEED + 2 * p + r]
                live = (jnp.minimum(at, 0) + 1).astype(F32)
                c = weights[jnp.maximum(at, 0)] * live
                here = slice(u * TILE, (u + 1) * TILE), slice(r * TILE, (r + 1) * TILE)
                dense[p, here[0], here[1]] = c
                cols.append((c + live) - c * s[here])
            rows.append(jnp.concatenate(cols, axis=1))
        return total + dot3(split(jnp.concatenate(rows, axis=0)), v, (1, 1))

    total = jnp.zeros((K, K), F32)
    for c in range(STEPS // 2):
        arrive(c, 1)
        for p in range(c * PAIRS // 2, (c + 1) * PAIRS // 2):
            total = begin(p, total)
    summer.last()

    gram_pair = split(gram[...])

    def globally(d, pair):
        return dot3(pair, gram_pair, (1, 0)) + RIDGE * d

    residual = total - globally(x, pair)
    direction = residual
    norm = jnp.sum(residual * residual, axis=1, keepdims=True)

    pair = split(direction)

    def scores(p):
        return dot3(pair, (high[p], low[p]), (1, 0))

    applied = globally(direction, pair)
    s = scores(0)
    for p in range(PAIRS):
        following = scores(p + 1) if p + 1 < PAIRS else None
        applied = applied + dot3(split(s * dense[p]), (high[p], low[p]), (1, 1))
        s = following
    step = norm / (jnp.sum(direction * applied, axis=1, keepdims=True) + EPS)
    x = x + step * direction
    residual = residual - step * applied
    following = jnp.sum(residual * residual, axis=1, keepdims=True)
    direction = residual + following / (norm + EPS) * direction
    norm = following

    pair = split(direction)
    bend = direction * globally(direction, pair)
    for p in range(PAIRS):
        s = scores(p)
        bend = bend + s * s * dense[p]
    step = norm / (jnp.sum(bend, axis=1, keepdims=True) + EPS)
    x = x + step * direction
    users[...] = x

    y, z = spot // SIDE, lax.rem(spot, SIDE)
    def turn(a, d):
        return lax.rem(a + (d + SIDE), SIDE)

    def block(dy, dz):
        return (turn(y, dy) * SIDE + turn(z, dz)) * CORES + core

    def neighbour(axis, way):
        d = 1 if way == 0 else -1
        return block(d, 0) if axis == 0 else block(0, d)

    def rows(half, bit):
        if bit is None:
            return pl.ds(half * HALF, HALF)
        return pl.ds(half * HALF + bit * BIT, BIT)

    def line(half, way, far):
        axis = half
        d = 0 if not far else (-1 if way == 0 else 1)
        at = block(d, 0) if axis == 0 else block(0, d)
        r = rows(half, way if far else None)
        src = users.at[r] if not far else boxes.at[at, r]
        return remote(
            src, boxes.at[at, r], line_sems.at[0, half, way, far], line_sems.at[1, half, way, far],
            neighbour(axis, way), node,
        )

    def cross(half, along, way, far):
        axis = 1 - half
        d = 0 if not far else (-1 if way == 0 else 1)
        at = block(along, d) if axis == 1 else block(d, along)
        r = rows(half, way if far else None)
        src = users.at[r] if (not far and along == 0) else boxes.at[at, r]
        return remote(
            src, boxes.at[at, r],
            cross_sems.at[0, half, along % SIDE, way, far], cross_sems.at[1, half, along % SIDE, way, far],
            neighbour(axis, way), node,
        )

    def sibling(half, along, over):
        at = block(along, over) if half == 0 else block(over, along)
        r = rows(half, None)
        src = users.at[r] if (along == 0 and over == 0) else boxes.at[at, r]
        i = (along % SIDE) * SIDE + over % SIDE
        return remote(
            src, boxes.at[at, r], sib_sems.at[0, half, i], sib_sems.at[1, half, i],
            spot * CORES + 1 - core, node,
        )

    own = pltpu.make_async_copy(users, boxes.at[wide], own_sems.at[0])
    own.start()
    for half in range(2):
        for way in range(2):
            line(half, way, 0).start()
    for half in range(2):
        for way in range(2):
            cross(half, 0, way, 0).start()
    for half in range(2):
        sibling(half, 0, 0).start()

    pair = split(x)
    part[...] = dot3(pair, pair, (0, 0))
    summer = LineSummer(part, user_gram, eight, along_y, along_z, line_sum_sems)
    summer.first()

    def come_from(way):
        return -1 if way == 0 else 1

    for way in range(2):
        for half in range(2):
            line(half, way, 0).wait_recv()
            line(half, way, 1).start()
            for w in range(2):
                cross(half, come_from(way), w, 0).start()
            sibling(half, come_from(way), 0).start()
    summer.second()
    for half in range(2):
        for way in range(2):
            line(half, way, 1).wait_recv()
        for w in range(2):
            cross(half, 2, w, 0).start()
        sibling(half, 2, 0).start()
    summer.third()
    for along in (0, -1, 1, 2):
        for half in range(2):
            for way in range(2):
                cross(half, along, way, 0).wait_recv()
                cross(half, along, way, 1).start()
                sibling(half, along, come_from(way)).start()
        if along == -1:
            summer.fourth()
    for along in (0, -1, 1, 2):
        for half in range(2):
            for way in range(2):
                cross(half, along, way, 1).wait_recv()
            sibling(half, along, 2).start()
    summer.last()
    for along in (0, -1, 1, 2):
        for half in range(2):
            for over in (0, -1, 1, 2):
                sibling(half, along, over).wait()
            for way in range(2):
                for far in range(2):
                    cross(half, along, way, far).wait_send()
    for half in range(2):
        for way in range(2):
            for far in range(2):
                line(half, way, far).wait_send()
    own.wait()

    for half in range(2):
        for way in range(2):
            each(0, STEPS, lambda c, half=half, way=way: pass_on(c, node, way, half).wait_send())
        for c in range(STEPS // 2):
            pass_on(2 * c, left, 0, half).wait_send()
            pass_on(2 * c + 1, right, 1, half).wait_send()
    for way in range(2):
        rows_relay(way).wait_send()
        rows_near(way).wait_send()
        rows_far(way).wait_send()
    each(1, WIDE, lambda k: ask(k).wait_send())
    for part_rank in range(2):
        each(1, WIDE, lambda k, part_rank=part_rank: serve(k, part_rank).wait_send())


def step(item, req, place, where, weights, user):
    vmem = pl.BlockSpec(memory_space=pltpu.VMEM)
    smem = pl.BlockSpec(memory_space=pltpu.SMEM)
    hbm = pl.BlockSpec(memory_space=pl.ANY)
    return pl.pallas_call(
        step_kernel,
        out_shape=[
            pltpu.VMEM((K, K), F32),
            pltpu.VMEM((K, K), F32),
            pltpu.VMEM((WIDE, K, K), F32),
            pltpu.VMEM((WIDE, 1, TILE), jnp.int32),
        ],
        in_specs=[hbm, vmem, smem, smem, hbm, hbm],
        out_specs=[vmem] * 4,
        scratch_shapes=[
            pltpu.VMEM((TILES, QUARTER, TILE), F32),
            pltpu.VMEM((SHARE, K, TILE), F32),
            pltpu.VMEM((2, SHARE // 2, QUARTER, TILE), F32),
            pltpu.VMEM((2, WIDE, 2, RANKS, TILE), F32),
            pltpu.VMEM((2 * WIDE, RANKS, TILE), F32),
            pltpu.VMEM((2 * WIDE, RANKS, TILE), F32),
            pltpu.SMEM((WIDE, 1, TILE), jnp.int32),
            pltpu.VMEM((PAIRS, K, 2 * TILE), F32),
            pltpu.VMEM((NB, TILE, TILE), F32),
            pltpu.VMEM((K, K), F32),
            pltpu.VMEM((K, K), F32),
            pltpu.VMEM((K, K), F32),
            pltpu.VMEM((PLANE, PART, K), F32),
            pltpu.VMEM((NODE * CORES, PART, K), F32),
            pltpu.VMEM((NODE * CORES, BAND, K), F32),
            pltpu.VMEM((SIDE, BAND, K), F32),
            pltpu.VMEM((SIDE, BAND, K), F32),
            pltpu.VMEM((PAIRS, K, 2 * TILE), BF16),
            pltpu.VMEM((PAIRS, K, 2 * TILE), BF16),
            pltpu.VMEM((PAIRS, K, 2 * TILE), F32),
            pltpu.SemaphoreType.DMA((3, 2, PLANE)),
            pltpu.SemaphoreType.DMA((4, 2, NODE * CORES)),
            pltpu.SemaphoreType.DMA((2, 3, 2)),
            pltpu.SemaphoreType.DMA((2, WIDE)),
            pltpu.SemaphoreType.DMA((2, 2, WIDE)),
            pltpu.SemaphoreType.DMA((2, 2, 2, 2, STEPS)),
            pltpu.SemaphoreType.DMA((2, 2, 2, 2)),
            pltpu.SemaphoreType.DMA((2, 2, SIDE, 2, 2)),
            pltpu.SemaphoreType.DMA((2, 2, PLANE)),
            pltpu.SemaphoreType.DMA((TILES,)),
            pltpu.SemaphoreType.DMA((2,)),
            pltpu.SemaphoreType.DMA((1,)),
            pltpu.SemaphoreType.DMA,
        ],
        compiler_params=pltpu.CompilerParams(
            collective_id=0, has_side_effects=True, vmem_limit_bytes=50 * 1024 * 1024
        ),
        name="step",
    )(item, req, place, where, weights, user)


def mask_kernel(rows, boxes, users_in, gram_in, users_new, user_gram, out, table, zeros, sems):
    scalars = pltpu.make_async_copy(rows, table, sems.at[WIDE + 2])
    scalars.start()
    users = pltpu.make_async_copy(users_in, users_new, sems.at[WIDE])
    gram = pltpu.make_async_copy(gram_in, user_gram, sems.at[WIDE + 1])
    users.start()
    gram.start()
    wide = lax.axis_index("wide")
    zeros[...] = jnp.zeros_like(zeros)
    scalars.wait()

    def begin(g):
        named = table[g, 0, 2 * wide] >= 0

        @pl.when(named)
        def _():
            pltpu.make_async_copy(boxes.at[g], out.at[0, g], sems.at[g]).start()

        @pl.when(jnp.logical_not(named))
        def _():
            pltpu.make_async_copy(zeros, out.at[0, g], sems.at[g]).start()

    each(0, WIDE, begin)
    each(0, WIDE, lambda g: pltpu.make_async_copy(zeros, out.at[0, g], sems.at[g]).wait())
    users.wait()
    gram.wait()


def mask(table, boxes, users, gram):
    return pl.pallas_call(
        mask_kernel,
        out_shape=[
            jax.ShapeDtypeStruct((K, K), F32),
            jax.ShapeDtypeStruct((K, K), F32),
            jax.ShapeDtypeStruct((1, WIDE, K, K), F32),
        ],
        in_specs=[pl.BlockSpec(memory_space=pltpu.VMEM)] * 4,
        out_specs=[pl.BlockSpec(memory_space=pl.ANY)] * 3,
        scratch_shapes=[
            pltpu.SMEM((WIDE, 1, TILE), jnp.int32),
            pltpu.VMEM((K, K), F32),
            pltpu.SemaphoreType.DMA((WIDE + 3,)),
        ],
        compiler_params=pltpu.CompilerParams(vmem_limit_bytes=10 * 1024 * 1024),
        name="mask",
    )(table, boxes, users, gram)


def body(item_factors, need_owner, need_slot, block_index, block_count, weights, user_old):
    req, place, where = plan(need_owner[:, 0], need_slot, block_index, block_count)
    users_new, user_gram, boxes, table = step(
        item_factors.T, req.reshape(1, TILE), place, where, weights, user_old
    )
    return tuple(mask(table, boxes, users_new, user_gram))


def solution(mesh):
    placed = (
        P("wide", "node"),
        P("wide", None),
        P("wide"),
        P(("wide", "node")),
        P(("wide", "node")),
        P(("wide", "node"), None, None),
        P(("wide", "node"), None),
    )
    return jax.shard_map(
        body,
        mesh=mesh,
        in_specs=placed,
        out_specs=(P(("wide", "node"), None), P(), P("wide", None, "node", None)),
        check_vma=False,
    )
```
